32 devices in a mesh: groups: 1, sector: 32 (over z, y, x, core).
Axes of the slice: x: 2, y: 2, z: 4, core: 2. Of those that a mesh axis runs over, the one named last changes fastest.
Arguments:
- wavefunction: bfloat16 [512, 128, 128], P(('groups', 'sector')), may hold values from -16 to 16
- onsite_energy: float32 [512], P(('groups', 'sector')), may hold values from 0.3 to 5
- left_env: bfloat16 [128, 32, 128, 128], P(('groups', 'sector')), may hold values from -0.09375 to 0.09375
- right_env: bfloat16 [128, 32, 128, 128], P(('groups', 'sector')), may hold values from -0.5 to 0.5
- source_device: int32 [512, 16], P(('groups', 'sector')), may hold values from 0 to 31, all different within a row; in each aligned block of 16 rows (0 to 15, 16 to 31, ...) at most 8 rows name the same one
- source_block: int32 [512, 16], P(('groups', 'sector')), may hold values from 0 to 15
Outputs:
- applied: bfloat16 [512, 128, 128], P(('groups', 'sector'))
- residual: bfloat16 [512, 128, 128], P(('groups', 'sector'))
- quotient: float32 [1], P('groups')
The draws below stay inside these ranges and needn't reach their ends.
Inputs may be any that keep to these rules, and one draw needn't show every extreme that they name: `source_device`: each row names 16 different devices; among the 16 rows of one device every device is named by exactly 8 rows.
All inputs are finite; a program needn't handle non-finite values.
Results may differ from the reference program's by a relative error of at most 0.004.
Values may be sent and summed in bfloat16 or wider, within the bound.
No kernel may reach another device: no remote copies, remote signals or barrier semaphores. Data moves between devices by JAX's collectives and lax.ppermute only.
A program may use at most 128 MiB of HBM per device.

```python
import math
import jax
import jax.numpy as jnp
import numpy as np
from jax import lax

BLOCK = 128
LEFT_SEC = 4
RIGHT_SEC = 4
LOCAL_CH = 16
HOPS = 16
CHANNELS = 32
SEC_DEV = 16
OWNERS = 32
CAP = 8
NSEC = 512
LEFT_ROWS = 128
RIGHT_ROWS = 128
N_SECTOR = 32


def hop_signs(key):
    bits = jax.random.randint(jax.random.fold_in(key, 77), (HOPS,), 0, 2)
    return (2 * bits - 1).astype(jnp.float32)


def channel_diagonal(key, local_value, hop_value):
    signs = hop_signs(key)
    return jnp.concatenate([jnp.full((LOCAL_CH,), local_value, jnp.float32), hop_value * signs])


def draw_wavefunction(key, part):
    key = jax.random.fold_in(key, 11)
    keys = jax.random.split(key, 4)
    base = jax.random.normal(keys[0], (NSEC, BLOCK, BLOCK), jnp.float32)
    common = jax.random.normal(keys[3], (1, BLOCK, BLOCK), jnp.float32)
    mixed = jnp.clip(0.75 * base + 0.65 * common, -4.5, 4.5)
    row_power = 0.5
    col_power = 0.5
    row_scale = 10.0 ** (row_power * jax.random.uniform(keys[1], (NSEC, BLOCK, 1), jnp.float32))
    col_scale = 10.0 ** (col_power * jax.random.uniform(keys[2], (NSEC, 1, BLOCK), jnp.float32))
    position = jnp.arange(NSEC, dtype=jnp.float32) / NSEC
    block_scale = (3.0 ** (0.5 * position))[:, None, None]
    return (0.2 * mixed * row_scale * col_scale * block_scale).astype(jnp.bfloat16)


def draw_onsite_energy(key, part):
    key = jax.random.fold_in(key, 23)
    position = jnp.arange(NSEC, dtype=jnp.float32) / NSEC
    factor = jax.random.uniform(key, (NSEC,), jnp.float32, 0.6, 1.4)
    return (0.5 + 3.0 * position) * factor


def draw_left_env(key, part):
    diagonal = channel_diagonal(key, 0.06, -0.06)
    key = jax.random.fold_in(key, 31)
    spread = (BLOCK * CHANNELS) ** (-0.5)
    noise = jnp.clip(jax.random.normal(key, (LEFT_ROWS, CHANNELS, BLOCK, BLOCK), jnp.float32), -3.0, 3.0) * spread
    identity = jnp.eye(BLOCK, dtype=jnp.float32)
    total = noise + diagonal[None, :, None, None] * identity[None, None]
    return jnp.clip(total, -0.09375, 0.09375).astype(jnp.bfloat16)


def draw_right_env(key, part):
    diagonal = channel_diagonal(key, 0.3, 0.3)
    key = jax.random.fold_in(key, 37)
    spread = BLOCK ** (-0.5)
    noise = jnp.clip(jax.random.normal(key, (RIGHT_ROWS, CHANNELS, BLOCK, BLOCK), jnp.float32), -3.0, 3.0) * spread
    identity = jnp.eye(BLOCK, dtype=jnp.float32)
    total = noise + diagonal[None, :, None, None] * identity[None, None]
    return jnp.clip(total, -0.5, 0.5).astype(jnp.bfloat16)


def plant(entries, rng, least, high):
    longest = entries.shape.index(max(entries.shape))
    spots = []
    for shift in (0, 1):
        where = [jax.random.randint(jax.random.fold_in(rng, axis), (), 0, length) for axis, length in enumerate(entries.shape)]
        where[longest] = (where[longest] + shift) % entries.shape[longest]
        spots.append(tuple(where))
    return entries.at[spots[0]].set(least).at[spots[1]].set(high)


def assign_block(key, own, number, rows, amount, top, reach, lean):
    ranking = jax.random.permutation(key, amount)
    crowded, usual = load_shares(amount, rows * top, reach, lean, True), load_shares(amount, rows * top, reach, lean, False)
    places = jnp.arange(amount)

    def named(tallies, rotation):
        used = int((tallies > 0).sum())
        fixed = max(1, used // 4)
        moved = fixed + (places - fixed + rotation * (used - fixed)) % max(1, amount - fixed)
        return jnp.zeros((amount,), jnp.int32).at[ranking[jnp.where(places < fixed, places, moved)]].set(jnp.asarray(tallies, jnp.int32))

    tallies = jnp.where(number % 4 == 0, named(crowded, number // 4), named(usual, number - number // 4 - 1))
    mixed = jax.random.permutation(jax.random.fold_in(own, 3), amount)
    giver, receiver = mixed[0:amount // 2 * 2:2], mixed[1:amount // 2 * 2:2]
    room = jnp.minimum(tallies[giver] - 1, reach - tallies[receiver]) // 2
    room = jnp.where((giver == ranking[0]) | (receiver == ranking[0]) | (tallies[receiver] == 0), 0, jnp.maximum(room, 0))
    moved = jax.random.randint(jax.random.fold_in(own, 4), (amount // 2,), 0, 1 << 20) % (room + 1)
    tallies = tallies.at[giver].add(-moved).at[receiver].add(moved)
    labels = jnp.searchsorted(jnp.cumsum(tallies), jnp.arange(rows * top), side="right").astype(jnp.int32)
    table = labels.reshape(top, rows).T
    table = table[jax.random.permutation(jax.random.fold_in(own, 1), rows)]
    rotation = jax.random.randint(jax.random.fold_in(own, 2), (rows, 1), 0, top)
    return jnp.take_along_axis(table, (jnp.arange(top)[None, :] + rotation) % top, axis=1)


def load_shares(amount, total, reach, skew, full):
    weights = [(1 << 20) // math.isqrt(rank ** skew) + 1 for rank in range(1, amount + 1)]
    largest = reach if full else min(reach, max(-(-total // amount), total * weights[0] // sum(weights)))
    least = 1 if total - largest >= amount - 1 else 0
    given, rest = [largest] + [least] * (amount - 1), total - largest - least * (amount - 1)
    while rest > 0:
        movable = [i for i in range(1, amount) if given[i] < largest] or [i for i in range(1, amount) if given[i] < reach]
        mass, budget = sum([weights[i] for i in movable]), rest
        for i in movable:
            more = min(reach - given[i], max(1, budget * weights[i] // mass), rest)
            given[i] = given[i] + more
            rest = rest - more
    return np.array(given)


def setup_inputs(seed: int = 0, part: int = 0) -> dict:
    key_of = jax.random.split(jax.random.key(seed), 7)
    part_splits = jax.random.split(jax.random.fold_in(key_of[6], part), 7)
    wavefunction = draw_wavefunction(jax.random.fold_in(jax.random.fold_in(key_of[6], part), 71), part)
    onsite_energy = draw_onsite_energy(jax.random.fold_in(jax.random.fold_in(key_of[6], part), 71), part)
    left_env = draw_left_env(jax.random.fold_in(jax.random.fold_in(key_of[6], part), 71), part)
    right_env = draw_right_env(jax.random.fold_in(jax.random.fold_in(key_of[6], part), 71), part)
    source_device_keys = jax.random.split(jax.random.fold_in(part_splits[4], 1), NSEC // SEC_DEV)
    source_device_turns = jax.random.permutation(jax.random.fold_in(part_splits[4], 3), NSEC // SEC_DEV)
    source_device = jax.vmap(lambda own, number: assign_block(jax.random.fold_in(part_splits[4], 2), own, number, SEC_DEV, OWNERS, HOPS, CAP, 0))(source_device_keys, source_device_turns).reshape((NSEC, HOPS))
    source_block = plant(jax.random.randint(part_splits[5], (NSEC, HOPS), 0, SEC_DEV), jax.random.fold_in(part_splits[5], 1), 0, SEC_DEV - 1).astype(jnp.int32)
    return {"wavefunction": wavefunction, "onsite_energy": onsite_energy, "left_env": left_env, "right_env": right_env, "source_device": source_device, "source_block": source_block}


def reference(wavefunction, onsite_energy, left_env, right_env, source_device, source_block):
    source = (source_device * SEC_DEV + source_block).astype(jnp.int32)
    source = source.reshape(N_SECTOR, SEC_DEV * HOPS)
    full_psi = wavefunction

    def per_device(inputs_one):
        block, energies, left_block, right_block, wanted = inputs_one
        blocks_grid = block.astype(jnp.float32).reshape(LEFT_SEC, RIGHT_SEC, BLOCK, BLOCK)
        fetched = full_psi[wanted].astype(jnp.float32).reshape(LEFT_SEC, RIGHT_SEC, HOPS, BLOCK, BLOCK)
        spread_out = jnp.broadcast_to(blocks_grid[:, :, None], (LEFT_SEC, RIGHT_SEC, LOCAL_CH, BLOCK, BLOCK))
        inputs_all = jnp.concatenate([spread_out, fetched], axis=2)
        middle = jnp.einsum("ijhab,jhbc->ijhac", inputs_all, right_block.astype(jnp.float32), precision=lax.Precision.HIGHEST)
        middle = lax.optimization_barrier(middle.astype(jnp.bfloat16)).astype(jnp.float32)
        summed = jnp.einsum("ihxa,ijhac->ijxc", left_block.astype(jnp.float32), middle, precision=lax.Precision.HIGHEST)
        return summed.reshape(SEC_DEV, BLOCK, BLOCK) + energies[:, None, None] * block.astype(jnp.float32)

    hpsi = lax.map(per_device, (
        wavefunction.reshape(N_SECTOR, SEC_DEV, BLOCK, BLOCK),
        onsite_energy.reshape(N_SECTOR, SEC_DEV),
        left_env.reshape(N_SECTOR, LEFT_SEC, CHANNELS, BLOCK, BLOCK),
        right_env.reshape(N_SECTOR, RIGHT_SEC, CHANNELS, BLOCK, BLOCK),
        source))
    hpsi = hpsi.reshape(NSEC, BLOCK, BLOCK)
    psi_float = wavefunction.astype(jnp.float32)
    numerator = jnp.sum(psi_float * hpsi)
    denominator = jnp.sum(psi_float * psi_float)
    quotient = numerator / denominator
    residual = (hpsi - quotient * psi_float).astype(jnp.bfloat16)
    return hpsi.astype(jnp.bfloat16), residual, quotient.reshape(1)
```

```python
import functools

import jax
import jax.numpy as jnp
from jax import lax
from jax.experimental import pallas as pl
from jax.experimental.pallas import tpu as pltpu
from jax.sharding import PartitionSpec as P

F32 = jnp.float32
BF16 = jnp.bfloat16
VMEM_BYTES = 48 * 1024 * 1024
ANY = pl.BlockSpec(memory_space=pl.ANY)
VMEM = pl.BlockSpec(memory_space=pltpu.VMEM)
SMEM = pl.BlockSpec(memory_space=pltpu.SMEM)
TOKEN = jax.ShapeDtypeStruct((8, 128), F32)


def dot(a, b):
    return jnp.dot(a, b, preferred_element_type=F32)


def earlier_count(targets):
    length = targets.shape[0]
    row_iota = lax.broadcasted_iota(jnp.int32, (length, length), 0)
    col_iota = lax.broadcasted_iota(jnp.int32, (length, length), 1)
    earlier = (targets[:, None] == targets[None, :]) & (col_iota < row_iota)
    return jnp.sum(earlier.astype(jnp.int32), axis=1)


def ask_and_send(wavefunction, onsite_energy, left_env, right_env, source_device, source_block):
    owners = lax.axis_size("sector")
    sec_dev, block_size = wavefunction.shape[:2]
    left_count, channels = left_env.shape[:2]
    right_count = right_env.shape[0]
    hop_count = source_device.shape[1]
    local_count = channels - hop_count
    capacity = sec_dev * hop_count // owners
    targets = source_device.reshape(-1)
    slot_index = targets * capacity + earlier_count(targets)
    asked_for = jnp.zeros((owners * capacity,), jnp.int32).at[slot_index].set(source_block.reshape(-1))
    asked_for = lax.all_to_all(asked_for.reshape(owners, capacity), "sector", 0, 0, tiled=True)
    received = lax.all_to_all(wavefunction[asked_for], "sector", 0, 0, tiled=True)
    fetched = received.reshape(owners * capacity, block_size, block_size)[slot_index]
    fetched = fetched.reshape(left_count, right_count, hop_count, block_size, block_size)
    grid = wavefunction.reshape(left_count, right_count, 1, block_size, block_size)
    spread_out = jnp.broadcast_to(grid, (left_count, right_count, local_count, block_size, block_size))
    inputs_all = jnp.concatenate([spread_out, fetched], axis=2)
    middle = jnp.einsum("ijhab,jhbc->ijhac", inputs_all, right_env, preferred_element_type=F32).astype(BF16)
    summed = jnp.einsum("ihxa,ijhac->ijxc", left_env, middle, preferred_element_type=F32)
    psi_float = wavefunction.astype(F32)
    hpsi = summed.reshape(sec_dev, block_size, block_size) + onsite_energy[:, None, None] * psi_float
    numerator, denominator = lax.psum((jnp.sum(psi_float * hpsi), jnp.sum(psi_float * psi_float)), "sector")
    quotient = numerator / denominator
    residual = (hpsi - quotient * psi_float).astype(BF16)
    return hpsi.astype(BF16), residual, quotient.reshape(1)


def local_kernel(onsite, psi, right, left, acc, square, token, r_buf, l_buf, middle, sems):
    token[...] = jnp.zeros(token.shape, F32)
    rows, cols, size = psi.shape[0], psi.shape[1], psi.shape[2]
    chans = r_buf.shape[1]
    r_copy = [pltpu.make_async_copy(right.at[j, pl.ds(0, chans)], r_buf.at[j], sems.at[0, j]) for j in range(cols)]
    l_copy = [pltpu.make_async_copy(left.at[i, pl.ds(0, chans)], l_buf.at[i], sems.at[1, i]) for i in range(rows)]
    for copy in r_copy + l_copy:
        copy.start()
    for j in range(cols):
        r_copy[j].wait()
        column = psi[:, j].reshape(rows * size, size)
        for h in range(chans):
            product = dot(column, r_buf[j, h]).astype(BF16)
            for i in range(rows):
                middle[i, pl.ds(h * size, size), pl.ds(j * size, size)] = product[i * size : (i + 1) * size]
    total = jnp.zeros((size, size), F32)
    for i in range(rows):
        l_copy[i].wait()
        wide = jnp.concatenate([l_buf[i, h] for h in range(chans)], axis=1)
        summed = dot(wide, middle[i])
        for j in range(cols):
            block = psi[i, j].astype(F32)
            acc[i * cols + j] = summed[:, j * size : (j + 1) * size] + onsite[i * cols + j] * block
            total += block * block
    square[...] = total


def local_call(onsite, psi, right, left, hops):
    sec, size = psi.shape[:2]
    rows, chans = left.shape[0], left.shape[1] - hops
    cols = right.shape[0]
    return pl.pallas_call(
        local_kernel,
        out_shape=(jax.ShapeDtypeStruct((sec, size, size), F32), jax.ShapeDtypeStruct((size, size), F32), TOKEN),
        in_specs=[SMEM, VMEM, ANY, ANY],
        out_specs=(VMEM, VMEM, VMEM),
        scratch_shapes=[
            pltpu.VMEM((cols, chans, size, size), BF16),
            pltpu.VMEM((rows, chans, size, size), BF16),
            pltpu.VMEM((rows, chans * size, cols * size), BF16),
            pltpu.SemaphoreType.DMA((2, max(rows, cols))),
        ],
        compiler_params=pltpu.CompilerParams(vmem_limit_bytes=VMEM_BYTES),
        cost_estimate=pl.CostEstimate(
            flops=4 * sec * chans * size**3, bytes_accessed=4 * (rows + cols) * chans * size * size, transcendentals=0
        ),
        name="local_channels",
    )(onsite, psi.reshape(rows, cols, size, size), right, left)


def hop_kernel(plan, first, last, capacity, hops, *refs):
    refs = list(refs)
    take = lambda n: [refs.pop(0) for _ in range(n)]
    order, *terms = take(3)
    envs = take(4)
    acc_in = take(1 if first else 2)
    base, pieces = plan
    bufs = take(1 + max(p[0] for owner in pieces for p in owner))
    psis = take(2) if last else []
    square = take(1)[0] if last else None
    acc_out = take(2)
    sums = take(1)[0]
    psi, r_buf, l_buf, acc, psi_sem, env_sem, acc_sem = refs
    count = len(pieces)
    skip = envs[0].shape[1] - hops
    env_copies = []
    for e in range(2):
        for f, buf in enumerate((r_buf, l_buf)):
            src = envs[2 * e + f]
            src = src.at[:, pl.ds(skip, hops)]
            env_copies.append(pltpu.make_async_copy(src, buf.at[e], env_sem.at[2 * e + f]))
    psi_copies = []
    for s, owner in enumerate(pieces):
        for operand, rows, at in owner:
            sem = psi_sem.at[len(psi_copies)]
            psi_copies.append(pltpu.make_async_copy(bufs[operand], psi.at[s, pl.ds(at, rows)], sem))
    acc_copies = [pltpu.make_async_copy(ref, acc.at[e], acc_sem.at[e]) for e, ref in enumerate(acc_in)]
    for copy in psi_copies + env_copies[:2] + acc_copies[:1] + env_copies[2:] + acc_copies[1:]:
        copy.start()
    if first:
        acc[1] = jnp.zeros(acc.shape[1:], F32)
    outs = [pltpu.make_async_copy(acc.at[e], acc_out[e], acc_sem.at[e]) for e in range(2)]
    rcols = r_buf.shape[2]
    for e in range(2):
        if e == 0:
            for copy in psi_copies:
                copy.wait()
        for copy in env_copies[2 * e : 2 * e + 2]:
            copy.wait()
        if e < len(acc_copies):
            acc_copies[e].wait()

        def owner_step(s, carry, e=e):
            slot = order[base + s] * capacity
            words = [terms[e][slot + r] for r in range(capacity)]
            mids = []
            for w in words:
                rr = (w >> 16) & 255
                mids.append(dot(psi[s, w & 255], r_buf[e, rr // rcols, rr % rcols]).astype(BF16))
            parts = []
            for w, mid in zip(words, mids):
                ll = w >> 24
                parts.append(dot(l_buf[e, ll // rcols, ll % rcols], mid))
            for w, part in zip(words, parts):
                t = (w >> 8) & 255
                acc[e, t] = acc[e, t] + part
            return carry

        lax.fori_loop(0, count, owner_step, 0)
        outs[e].start()
    if last:
        total = jnp.zeros(acc.shape[2:], F32)
        for e in range(2):
            total = lax.fori_loop(
                0, acc.shape[1], lambda t, v, e=e: v + psis[e][t].astype(F32) * acc[e, t], total
            )
        lanes = lax.broadcasted_iota(jnp.int32, sums.shape, 1)
        sums[...] = jnp.where(lanes < sums.shape[1] // 2, jnp.sum(total), jnp.sum(square[...]))
    else:
        sums[...] = jnp.zeros(sums.shape, F32)
    for copy in outs:
        copy.wait()


def hop_call(name, order, terms, envs, accs, plan, bufs, last_args, owners, capacity, hops):
    sec, size = accs[0].shape[:2]
    first, last = len(accs) == 1, bool(last_args)
    count = len(plan[1])
    n_pieces = sum(len(owner) for owner in plan[1])
    rcols = hops
    acc_shape = jax.ShapeDtypeStruct((sec, size, size), F32)
    out_shape = (acc_shape, acc_shape)
    out_specs = (ANY, ANY)
    out_shape += (jax.ShapeDtypeStruct((owners, size), F32) if last else TOKEN,)
    out_specs += (VMEM,)
    n_front = 3 + len(envs)
    return pl.pallas_call(
        functools.partial(hop_kernel, plan, first, last, capacity, hops),
        out_shape=out_shape,
        in_specs=[SMEM] * 3 + [ANY] * (len(envs) + len(accs) + len(bufs)) + [VMEM] * len(last_args),
        out_specs=out_specs,
        scratch_shapes=[
            pltpu.VMEM((count, sec, size, size), BF16),
            pltpu.VMEM((2, envs[0].shape[0], rcols, size, size), BF16),
            pltpu.VMEM((2, envs[1].shape[0], rcols, size, size), BF16),
            pltpu.VMEM((2, sec, size, size), F32),
            pltpu.SemaphoreType.DMA((n_pieces,)),
            pltpu.SemaphoreType.DMA((4,)),
            pltpu.SemaphoreType.DMA((2,)),
        ],
        input_output_aliases={n_front + i: i for i in range(len(accs))},
        compiler_params=pltpu.CompilerParams(vmem_limit_bytes=VMEM_BYTES),
        cost_estimate=pl.CostEstimate(
            flops=8 * count * capacity * size**3, bytes_accessed=12 * 1024 * 1024, transcendentals=0
        ),
        name=name,
    )(order, *terms, *envs, *accs, *bufs, *last_args)


def finish_kernel(sums, psi, mine, theirs, applied, residual, quotient):
    lanes = lax.broadcasted_iota(jnp.int32, sums.shape, 1)
    half = sums.shape[1] // 2
    ratio = jnp.sum(jnp.where(lanes == 0, sums[...], 0.0)) / jnp.sum(jnp.where(lanes == half, sums[...], 0.0))
    hpsi = mine[...] + theirs[...]
    applied[...] = hpsi.astype(BF16)
    residual[...] = (hpsi - ratio * psi[...].astype(F32)).astype(BF16)
    quotient[0] = ratio


def finish_call(sums, psi, mine, theirs):
    sec, size = psi.shape[:2]
    step = sec // 4 if sec % 4 == 0 else sec
    block = pl.BlockSpec((step, size, size), lambda g: (g, 0, 0))
    return pl.pallas_call(
        finish_kernel,
        grid=(sec // step,),
        out_shape=(
            jax.ShapeDtypeStruct(psi.shape, BF16),
            jax.ShapeDtypeStruct(psi.shape, BF16),
            jax.ShapeDtypeStruct((1,), F32),
        ),
        in_specs=[pl.BlockSpec(sums.shape, lambda g: (0, 0)), block, block, block],
        out_specs=(block, block, SMEM),
        name="finish",
    )(sums, psi, mine, theirs)


def term_words(source_device, source_block, rows, cols, capacity):
    sec, hops = source_device.shape
    targets = source_device.reshape(-1)
    slots = targets * capacity + earlier_count(targets)
    index = jnp.arange(sec * hops, dtype=jnp.int32)
    t, k = index // hops, index % hops
    words = source_block.reshape(-1) | (t << 8) | (((t % cols) * hops + k) << 16) | (((t // cols) * hops + k) << 24)
    hit = slots[None, :] == index[:, None]
    return jnp.sum(jnp.where(hit, words[None, :], 0), axis=1)


def tie(value, *after):
    return lax.optimization_barrier((value,) + after)[0]


def spread_everywhere(wavefunction, onsite_energy, left_env, right_env, source_device, source_block):
    owners = lax.axis_size("sector")
    sec = wavefunction.shape[0]
    rows, cols = left_env.shape[0], right_env.shape[0]
    hops = source_device.shape[1]
    chans = left_env.shape[1] - hops
    capacity = sec * hops // owners

    def swap(value, mask):
        return lax.ppermute(value, "sector", [(i, i ^ mask) for i in range(owners)])

    core, x, y = 1, 2, 4
    far_masks = list(range(8, owners, 8))
    far = [swap(wavefunction, mask) for mask in far_masks]
    terms = term_words(source_device, source_block, rows, cols, capacity)
    terms_sib = swap(terms, core)
    psi_sib = swap(wavefunction, core)
    right_sib = swap(right_env, core)
    left_sib = swap(left_env, core)
    acc, square, token = local_call(onsite_energy, wavefunction, right_env, left_env, hops)
    accs = (acc,)
    envs = (right_env, left_env, right_sib, left_sib)
    blocks = list(zip([0] + far_masks, [wavefunction] + far))
    tokens = [token]
    out = None

    def run(group, last_args=(), ahead=None):
        nonlocal accs, out
        masks = jnp.array([mask for mask, _ in group], jnp.int32)
        order = lax.axis_index("sector") ^ masks
        if ahead is not None:
            order = tie(order, ahead)
        plan = (0, [[(s, sec, 0)] for s in range(len(group))])
        bufs = tuple(value for _, value in group)
        name = f"hops_{len(tokens)}"
        out = hop_call(name, order, (terms, terms_sib), envs, accs, plan, bufs, last_args, owners, capacity, hops)
        accs = out[:2]
        tokens.append(out[2])

    late = []
    tail = []
    arrived = []
    for g, (mask, block) in enumerate(blocks):
        final = g >= len(blocks) - 2
        if g == 1:
            block = tie(block, tokens[0])
        elif g > 1:
            block = tie(block, *arrived[g - 2], tokens[g - 2])
        from_x, from_y = swap(block, x), swap(block, y)
        relay = from_y if g % 2 == 0 else from_x
        if final:
            relay = tie(relay, tokens[len(blocks) - 2])
        diag = swap(relay, x if g % 2 == 0 else y)
        arrived.append((from_x, from_y))
        near = [(mask, block), (mask ^ x, from_x), (mask ^ y, from_y)]
        if final:
            late += near
            tail.append((mask ^ x ^ y, diag))
        else:
            run(near + [(mask ^ x ^ y, diag)], (), blocks[g + 2][1])
    run(late)
    run(tail, (wavefunction, psi_sib, square))
    sums = lax.all_to_all(out[2], "sector", 0, 0, tiled=True)
    theirs = swap(accs[1], core)
    return finish_call(sums, wavefunction, accs[0], theirs)


def local(wavefunction, onsite_energy, left_env, right_env, source_device, source_block):
    owners = lax.axis_size("sector")
    sec, hops = source_device.shape
    fits = owners >= 32 and owners & (owners - 1) == 0 and sec % 2 == 0 and sec < 128
    fits = fits and max(left_env.shape[0], right_env.shape[0]) * hops < 128
    plan = spread_everywhere if fits and 2 * (sec * hops // owners) >= sec else ask_and_send
    return plan(wavefunction, onsite_energy, left_env, right_env, source_device, source_block)


def solution(mesh):
    return jax.shard_map(
        local,
        mesh=mesh,
        in_specs=(
            P(("groups", "sector"), None, None),
            P(("groups", "sector")),
            P(("groups", "sector"), None, None, None),
            P(("groups", "sector"), None, None, None),
            P(("groups", "sector"), None),
            P(("groups", "sector"), None),
        ),
        out_specs=(
            P(("groups", "sector"), None, None),
            P(("groups", "sector"), None, None),
            P("groups"),
        ),
        check_vma=False,
    )
```

```python
import functools

import jax
import jax.numpy as jnp
from jax import lax
from jax.experimental import pallas as pl
from jax.experimental.pallas import tpu as pltpu
from jax.sharding import PartitionSpec as P

F32 = jnp.float32
BF16 = jnp.bfloat16
VMEM_BYTES = 16 * 1024 * 1024
LOCAL_BYTES = 48 * 1024 * 1024
FIRST_BYTES = 24 * 1024 * 1024
COST = pl.CostEstimate(flops=1, bytes_accessed=1, transcendentals=0)
ANY = pl.BlockSpec(memory_space=pl.ANY)
VMEM = pl.BlockSpec(memory_space=pltpu.VMEM)
HBM = pl.BlockSpec(memory_space=pltpu.HBM)
SMEM = pl.BlockSpec(memory_space=pltpu.SMEM)
TOKEN = jax.ShapeDtypeStruct((8, 128), F32)


def dot(a, b):
    return jnp.dot(a, b, preferred_element_type=F32)


def earlier_count(targets):
    length = targets.shape[0]
    row_iota = lax.broadcasted_iota(jnp.int32, (length, length), 0)
    col_iota = lax.broadcasted_iota(jnp.int32, (length, length), 1)
    earlier = (targets[:, None] == targets[None, :]) & (col_iota < row_iota)
    return jnp.sum(earlier.astype(jnp.int32), axis=1)


def ask_and_send(wavefunction, onsite_energy, left_env, right_env, source_device, source_block):
    owners = lax.axis_size("sector")
    sec_dev, block_size = wavefunction.shape[:2]
    left_count, channels = left_env.shape[:2]
    right_count = right_env.shape[0]
    hop_count = source_device.shape[1]
    local_count = channels - hop_count
    capacity = sec_dev * hop_count // owners
    targets = source_device.reshape(-1)
    slot_index = targets * capacity + earlier_count(targets)
    asked_for = jnp.zeros((owners * capacity,), jnp.int32).at[slot_index].set(source_block.reshape(-1))
    asked_for = lax.all_to_all(asked_for.reshape(owners, capacity), "sector", 0, 0, tiled=True)
    received = lax.all_to_all(wavefunction[asked_for], "sector", 0, 0, tiled=True)
    fetched = received.reshape(owners * capacity, block_size, block_size)[slot_index]
    fetched = fetched.reshape(left_count, right_count, hop_count, block_size, block_size)
    grid = wavefunction.reshape(left_count, right_count, 1, block_size, block_size)
    spread_out = jnp.broadcast_to(grid, (left_count, right_count, local_count, block_size, block_size))
    inputs_all = jnp.concatenate([spread_out, fetched], axis=2)
    middle = jnp.einsum("ijhab,jhbc->ijhac", inputs_all, right_env, preferred_element_type=F32).astype(BF16)
    summed = jnp.einsum("ihxa,ijhac->ijxc", left_env, middle, preferred_element_type=F32)
    psi_float = wavefunction.astype(F32)
    hpsi = summed.reshape(sec_dev, block_size, block_size) + onsite_energy[:, None, None] * psi_float
    numerator, denominator = lax.psum((jnp.sum(psi_float * hpsi), jnp.sum(psi_float * psi_float)), "sector")
    quotient = numerator / denominator
    residual = (hpsi - quotient * psi_float).astype(BF16)
    return hpsi.astype(BF16), residual, quotient.reshape(1)


def local_kernel(onsite, psi, right, left, acc, square, hop_env, r_buf, l_buf, middle, sems):
    rows, cols, size = psi.shape[0], psi.shape[1], psi.shape[2]
    chans = r_buf.shape[1]
    r_copy = [pltpu.make_async_copy(right.at[j, pl.ds(0, chans)], r_buf.at[j], sems.at[0, j]) for j in range(cols)]
    l_copy = [pltpu.make_async_copy(left.at[i, pl.ds(0, chans)], l_buf.at[i], sems.at[1, i]) for i in range(rows)]
    hop_copy = []
    for n in range(cols + rows):
        env, row = (right, n) if n < cols else (left, n - cols)
        src = env.at[row, pl.ds(chans, hop_env.shape[1])]
        hop_copy.append(pltpu.make_async_copy(src, hop_env.at[n], sems.at[2 + n // cols, n % cols]))
    for copy in r_copy + l_copy + hop_copy:
        copy.start()
    for j in range(cols):
        r_copy[j].wait()
        column = psi[:, j].reshape(rows * size, size)
        for h in range(chans):
            product = dot(column, r_buf[j, h]).astype(BF16)
            for i in range(rows):
                middle[i, pl.ds(h * size, size), pl.ds(j * size, size)] = product[i * size : (i + 1) * size]
    total = jnp.zeros((size, size), F32)
    for i in range(rows):
        l_copy[i].wait()
        wide = jnp.concatenate([l_buf[i, h] for h in range(chans)], axis=1)
        summed = dot(wide, middle[i])
        for j in range(cols):
            block = psi[i, j].astype(F32)
            acc[i * cols + j] = summed[:, j * size : (j + 1) * size] + onsite[i * cols + j] * block
            total += block * block
    square[...] = total
    for copy in hop_copy:
        copy.wait()


def local_call(onsite, psi, right, left, hops):
    sec, size = psi.shape[:2]
    rows, cols, chans = left.shape[0], right.shape[0], left.shape[1] - hops
    return pl.pallas_call(
        local_kernel,
        out_shape=(
            jax.ShapeDtypeStruct((sec, size, size), F32),
            jax.ShapeDtypeStruct((size, size), F32),
            jax.ShapeDtypeStruct((cols + rows, hops, size, size), BF16),
        ),
        in_specs=[SMEM, VMEM, HBM, HBM],
        out_specs=[VMEM] * 3,
        scratch_shapes=[
            pltpu.VMEM((cols, chans, size, size), BF16),
            pltpu.VMEM((rows, chans, size, size), BF16),
            pltpu.VMEM((rows, chans * size, cols * size), BF16),
            pltpu.SemaphoreType.DMA((4, max(rows, cols))),
        ],
        compiler_params=pltpu.CompilerParams(vmem_limit_bytes=LOCAL_BYTES),
        cost_estimate=COST,
        name="local_channels",
    )(onsite, psi.reshape(rows, cols, size, size), right, left)


def hop_kernel(base, count, first, last, capacity, *refs):
    refs = list(refs)
    take = lambda n: [refs.pop(0) for _ in range(n)]
    order, *terms = take(3)
    envs = take(2) if first else take(1)
    acc_in = take(1 if first else 2)
    bufs = take(count)
    psis = take(2) if last else []
    square = take(1)[0] if last else None
    acc = take(2)
    sums = take(1)[0]
    env = take(1)[0] if first else envs[0]
    psi, sems, env_sems = refs
    hops, rows = env.shape[2], env.shape[1] // 2
    copies = [pltpu.make_async_copy(buf, psi.at[s], sems.at[s]) for s, buf in enumerate(bufs)]
    fills = []
    if first:
        for e in range(2):
            for f in range(2):
                half = pl.ds(f * rows, rows)
                fills.append(pltpu.make_async_copy(envs[e].at[half], env.at[e, half], env_sems.at[2 * e + f]))
    for copy in copies + fills:
        copy.start()
    for e in range(2):
        acc[e][...] = acc_in[e][...] if e < len(acc_in) else jnp.zeros(acc[e].shape, F32)
    for copy in copies:
        copy.wait()
    for e in range(2):
        for fill in fills[2 * e : 2 * e + 2]:
            fill.wait()

        def owner_step(s, carry, e=e):
            slot = order[base + s] * capacity
            words = [terms[e][slot + r] for r in range(capacity)]
            mids = []
            for w in words:
                right = (w >> 16) & 255
                mids.append(dot(psi[s, w & 255], env[e, right // hops, right % hops]).astype(BF16))
            parts = []
            for w, mid in zip(words, mids):
                left = w >> 24
                parts.append(dot(env[e, left // hops, left % hops], mid))
            for w, part in zip(words, parts):
                t = (w >> 8) & 255
                acc[e][t] = acc[e][t] + part
            return carry

        lax.fori_loop(0, count, owner_step, 0)
    if last:
        total = jnp.zeros(acc[0].shape[1:], F32)
        for e in range(2):
            total = lax.fori_loop(
                0, acc[e].shape[0], lambda t, v, e=e: v + psis[e][t].astype(F32) * acc[e][t], total
            )
        lanes = lax.broadcasted_iota(jnp.int32, sums.shape, 1)
        sums[...] = jnp.where(lanes < sums.shape[1] // 2, jnp.sum(total), jnp.sum(square[...]))
    else:
        sums[...] = jnp.zeros(sums.shape, F32)


def hop_call(name, order, base, terms, envs, accs, bufs, last_args, owners, capacity):
    sec, size = accs[0].shape[:2]
    first, last = len(accs) == 1, bool(last_args)
    count = len(bufs)
    acc_shape = jax.ShapeDtypeStruct((sec, size, size), F32)
    out_shape = [acc_shape, acc_shape, jax.ShapeDtypeStruct((owners, size), F32) if last else TOKEN]
    if first:
        out_shape.append(jax.ShapeDtypeStruct((2,) + envs[0].shape, BF16))
    return pl.pallas_call(
        functools.partial(hop_kernel, base, count, first, last, capacity),
        out_shape=out_shape,
        in_specs=[SMEM] * 3
        + [HBM if first else VMEM] * len(envs)
        + [VMEM] * len(accs)
        + [ANY] * count
        + [VMEM] * len(last_args),
        out_specs=[VMEM] * len(out_shape),
        scratch_shapes=[
            pltpu.VMEM((count, sec, size, size), BF16),
            pltpu.SemaphoreType.DMA((count,)),
            pltpu.SemaphoreType.DMA((4,)),
        ],
        compiler_params=pltpu.CompilerParams(vmem_limit_bytes=FIRST_BYTES if first else VMEM_BYTES),
        cost_estimate=COST,
        name=name,
    )(order, *terms, *envs, *accs, *bufs, *last_args)


def hold_until(values, tokens):
    count = len(values)
    return pl.pallas_call(
        lambda *refs: None,
        out_shape=[jax.ShapeDtypeStruct(value.shape, value.dtype) for value in values],
        in_specs=[ANY] * (count + len(tokens)),
        out_specs=[ANY] * count,
        input_output_aliases={n: n for n in range(count)},
        compiler_params=pltpu.CompilerParams(vmem_limit_bytes=VMEM_BYTES),
        cost_estimate=COST,
        name="hold",
    )(*values, *tokens)


def finish_kernel(sums, psi, mine, theirs, applied, residual, quotient):
    lanes = lax.broadcasted_iota(jnp.int32, sums.shape, 1)
    half = sums.shape[1] // 2
    ratio = jnp.sum(jnp.where(lanes == 0, sums[...], 0.0)) / jnp.sum(jnp.where(lanes == half, sums[...], 0.0))
    quotient[0] = ratio
    for t in range(psi.shape[0]):
        hpsi = mine[t] + theirs[t]
        applied[t] = hpsi.astype(BF16)
        residual[t] = (hpsi - ratio * psi[t].astype(F32)).astype(BF16)


def finish_call(sums, psi, mine, theirs):
    shape = jax.ShapeDtypeStruct(psi.shape, BF16)
    return pl.pallas_call(
        finish_kernel,
        out_shape=(shape, shape, jax.ShapeDtypeStruct((1,), F32)),
        in_specs=[VMEM] * 4,
        out_specs=(VMEM, VMEM, SMEM),
        compiler_params=pltpu.CompilerParams(vmem_limit_bytes=VMEM_BYTES),
        name="finish",
    )(sums, psi, mine, theirs)


def term_words(source_device, source_block, cols, capacity):
    sec, hops = source_device.shape
    targets = source_device.reshape(-1)
    slots = targets * capacity + earlier_count(targets)
    index = jnp.arange(sec * hops, dtype=jnp.int32)
    t, k = index // hops, index % hops
    right, left = (t % cols) * hops + k, (cols + t // cols) * hops + k
    words = source_block.reshape(-1) | (t << 8) | (right << 16) | (left << 24)
    hit = slots[None, :] == index[:, None]
    return jnp.sum(jnp.where(hit, words[None, :], 0), axis=1)


def spread_everywhere(wavefunction, onsite_energy, left_env, right_env, source_device, source_block):
    owners = lax.axis_size("sector")
    sec = wavefunction.shape[0]
    hops = source_device.shape[1]
    capacity = sec * hops // owners
    core, x, y, z = 1, 2, 4, 8
    xy = x ^ y
    layers = owners // z

    def swap(value, mask):
        return lax.ppermute(value, "sector", [(i, i ^ mask) for i in range(owners)])

    def swap_middle(value):
        pairs = []
        for i in range(owners):
            layer = i // z
            to = layers - 1 - layer if layer in (1, 2) else layer
            pairs.append((i, to * z + i % z))
        return lax.ppermute(value, "sector", pairs)

    me = lax.axis_index("sector")
    outer = (me < z) | (me >= owners - z)
    layer_masks = [0, z, jnp.where(outer, 2 * z, 3 * z), jnp.where(outer, 3 * z, 2 * z)]
    groups = [
        [(0, 0), (0, x), (0, y), (1, 0)],
        [(1, x), (1, y)],
        [(0, xy), (1, xy), (2, 0)],
        [(2, x), (2, y), (3, 0)],
        [(3, x), (3, y)],
        [(2, xy), (3, xy)],
    ]
    order = jnp.stack([me ^ layer_masks[b] ^ bits for group in groups for b, bits in group])

    held = {(0, 0): wavefunction}
    state = {"base": 0}

    def hold(keys, *tokens):
        held.update(zip(keys, hold_until([held[key] for key in keys], tokens)))

    def run(group, last_args=()):
        first = len(state["accs"]) == 1
        out = hop_call(
            f"hops_{group}", order, state["base"], terms, state["envs"], state["accs"],
            tuple(held[key] for key in groups[group]), last_args, owners, capacity,
        )
        state["accs"] = out[:2]
        state["base"] += len(groups[group])
        if first:
            state["envs"] = out[3:]
        return out[2]

    held[1, 0] = swap(wavefunction, z)
    held["middle"] = swap_middle(wavefunction)
    held[0, x], held[0, y] = swap(wavefunction, x), swap(wavefunction, y)
    terms = term_words(source_device, source_block, right_env.shape[0], capacity)
    terms = (terms, swap(terms, core))
    acc, square, held["env"] = local_call(onsite_energy, wavefunction, right_env, left_env, hops)
    hold([(1, 0), "middle", (0, x), (0, y), "env"], terms[1])

    for link in (x, y):
        held[1, link] = swap(held[1, 0], link)
    held["outer"] = swap(held["middle"], z)
    held["middle_2"] = swap_middle(held[1, 0])
    env_sib = swap(held["env"], core)
    hold([(0, y)], env_sib)
    state["accs"], state["envs"] = (acc,), (held["env"], env_sib)

    held[0, xy] = swap(held[0, y], x)
    done = run(0)
    hold([(1, x), (1, y), "outer", "middle_2"], done)
    held[1, xy] = swap(held[1, x], y)
    held["outer_2"] = swap(held["middle_2"], z)
    held[2, 0] = jnp.where(outer, held["outer"], held["middle"])
    for link in (x, y):
        held[2, link] = swap(held[2, 0], link)
    done = run(1)
    hold([(0, xy), (1, xy), "outer_2"], done)
    held[3, 0] = jnp.where(outer, held["outer_2"], held["middle_2"])
    for link in (x, y):
        held[3, link] = swap(held[3, 0], link)
    done = run(2)
    hold([(2, x), (2, y)], done)
    held[2, xy] = swap(held[2, y], x)
    done = run(3)
    hold([(3, x)], done)
    held[3, xy] = swap(held[3, x], y)
    run(4)
    psi_sib = swap(wavefunction, core)
    sums = run(5, (wavefunction, psi_sib, square))
    sums = lax.all_to_all(sums, "sector", 0, 0, tiled=True)
    mine, theirs = state["accs"]
    return finish_call(sums, wavefunction, mine, swap(theirs, core))


def local(wavefunction, onsite_energy, left_env, right_env, source_device, source_block):
    owners = lax.axis_size("sector")
    sec, hops = source_device.shape
    fits = owners == 32 and sec <= 256 and (left_env.shape[0] + right_env.shape[0]) * hops <= 128
    plan = spread_everywhere if fits and 2 * (sec * hops // owners) >= sec else ask_and_send
    return plan(wavefunction, onsite_energy, left_env, right_env, source_device, source_block)


def solution(mesh):
    return jax.shard_map(
        local,
        mesh=mesh,
        in_specs=(
            P(("groups", "sector"), None, None),
            P(("groups", "sector")),
            P(("groups", "sector"), None, None, None),
            P(("groups", "sector"), None, None, None),
            P(("groups", "sector"), None),
            P(("groups", "sector"), None),
        ),
        out_specs=(
            P(("groups", "sector"), None, None),
            P(("groups", "sector"), None, None),
            P("groups"),
        ),
        check_vma=False,
    )
```

```python
import functools

import jax
import jax.numpy as jnp
from jax import lax
from jax.experimental import pallas as pl
from jax.experimental.pallas import tpu as pltpu
from jax.sharding import PartitionSpec as P

F32 = jnp.float32
BF16 = jnp.bfloat16
VMEM_BYTES = 16 * 1024 * 1024
LOCAL_BYTES = 50 * 1024 * 1024
COST = pl.CostEstimate(flops=1, bytes_accessed=1, transcendentals=0)
ANY = pl.BlockSpec(memory_space=pl.ANY)
VMEM = pl.BlockSpec(memory_space=pltpu.VMEM)
HBM = pl.BlockSpec(memory_space=pltpu.HBM)
SMEM = pl.BlockSpec(memory_space=pltpu.SMEM)
TOKEN = jax.ShapeDtypeStruct((8, 128), F32)


def dot(a, b):
    return jnp.dot(a, b, preferred_element_type=F32)


def earlier_count(targets):
    length = targets.shape[0]
    row_iota = lax.broadcasted_iota(jnp.int32, (length, length), 0)
    col_iota = lax.broadcasted_iota(jnp.int32, (length, length), 1)
    earlier = (targets[:, None] == targets[None, :]) & (col_iota < row_iota)
    return jnp.sum(earlier.astype(jnp.int32), axis=1)


def ask_and_send(wavefunction, onsite_energy, left_env, right_env, source_device, source_block):
    owners = lax.axis_size("sector")
    sec_dev, block_size = wavefunction.shape[:2]
    left_count, channels = left_env.shape[:2]
    right_count = right_env.shape[0]
    hop_count = source_device.shape[1]
    local_count = channels - hop_count
    capacity = sec_dev * hop_count // owners
    targets = source_device.reshape(-1)
    slot_index = targets * capacity + earlier_count(targets)
    asked_for = jnp.zeros((owners * capacity,), jnp.int32).at[slot_index].set(source_block.reshape(-1))
    asked_for = lax.all_to_all(asked_for.reshape(owners, capacity), "sector", 0, 0, tiled=True)
    received = lax.all_to_all(wavefunction[asked_for], "sector", 0, 0, tiled=True)
    fetched = received.reshape(owners * capacity, block_size, block_size)[slot_index]
    fetched = fetched.reshape(left_count, right_count, hop_count, block_size, block_size)
    grid = wavefunction.reshape(left_count, right_count, 1, block_size, block_size)
    spread_out = jnp.broadcast_to(grid, (left_count, right_count, local_count, block_size, block_size))
    inputs_all = jnp.concatenate([spread_out, fetched], axis=2)
    middle = jnp.einsum("ijhab,jhbc->ijhac", inputs_all, right_env, preferred_element_type=F32).astype(BF16)
    summed = jnp.einsum("ihxa,ijhac->ijxc", left_env, middle, preferred_element_type=F32)
    psi_float = wavefunction.astype(F32)
    hpsi = summed.reshape(sec_dev, block_size, block_size) + onsite_energy[:, None, None] * psi_float
    numerator, denominator = lax.psum((jnp.sum(psi_float * hpsi), jnp.sum(psi_float * psi_float)), "sector")
    quotient = numerator / denominator
    residual = (hpsi - quotient * psi_float).astype(BF16)
    return hpsi.astype(BF16), residual, quotient.reshape(1)


def local_kernel(onsite, psi, right, left, acc, square, moved, onsite_buf, psi_buf, r_buf, l_buf, middle, sems, moved_sems):
    rows, cols, size = psi.shape[0], psi.shape[1], psi.shape[2]
    chans = r_buf.shape[1]
    hops = right.shape[1] - chans
    copies = [pltpu.make_async_copy(psi, psi_buf, sems.at[0, 0]), pltpu.make_async_copy(onsite, onsite_buf, sems.at[0, 1])]
    r_copy = [pltpu.make_async_copy(right.at[j, pl.ds(0, chans)], r_buf.at[j], sems.at[1, j]) for j in range(cols)]
    l_copy = [pltpu.make_async_copy(left.at[i, pl.ds(0, chans)], l_buf.at[i], sems.at[2, i]) for i in range(rows)]
    parts = [right.at[j, pl.ds(chans, hops)] for j in range(cols)] + [left.at[i, pl.ds(chans, hops)] for i in range(rows)]
    for n, part in enumerate(parts):
        parts[n] = pltpu.make_async_copy(part, moved.at[pl.ds(n * hops, hops)], moved_sems.at[n])
    for copy in copies + r_copy + l_copy:
        copy.start()
    for copy in copies:
        copy.wait()
    for j in range(cols):
        r_copy[j].wait()
        if j == 1:
            for part in parts:
                part.start()
        column = psi_buf[:, j].reshape(rows * size, size)
        for h in range(0, chans, 2):
            pair = jnp.concatenate([r_buf[j, h], r_buf[j, h + 1]], axis=1)
            product = dot(column, pair).astype(BF16)
            for i in range(rows):
                for g in range(2):
                    block = product[i * size : (i + 1) * size, g * size : (g + 1) * size]
                    middle[i, pl.ds((h + g) * size, size), pl.ds(j * size, size)] = block
    total = jnp.zeros((size, size), F32)
    first = (rows + cols) * hops
    for i in range(rows):
        l_copy[i].wait()
        wide = jnp.concatenate([l_buf[i, h] for h in range(chans)], axis=1)
        summed = dot(wide, middle[i])
        for j in range(cols):
            moved[first + i * cols + j] = psi_buf[i, j]
            block = psi_buf[i, j].astype(F32)
            acc[i * cols + j] = summed[:, j * size : (j + 1) * size] + onsite_buf[i * cols + j] * block
            total += block * block
    square[...] = total
    for part in parts:
        part.wait()


def local_call(onsite, psi, right, left, hops):
    sec, size = psi.shape[:2]
    rows, cols, chans = left.shape[0], right.shape[0], left.shape[1] - hops
    return pl.pallas_call(
        local_kernel,
        out_shape=(
            jax.ShapeDtypeStruct((sec, size, size), F32),
            jax.ShapeDtypeStruct((size, size), F32),
            jax.ShapeDtypeStruct(((rows + cols) * hops + sec, size, size), BF16),
        ),
        in_specs=[HBM] * 4,
        out_specs=[VMEM] * 3,
        scratch_shapes=[
            pltpu.SMEM((sec,), F32),
            pltpu.VMEM((rows, cols, size, size), BF16),
            pltpu.VMEM((cols, chans, size, size), BF16),
            pltpu.VMEM((rows, chans, size, size), BF16),
            pltpu.VMEM((rows, chans * size, cols * size), BF16),
            pltpu.SemaphoreType.DMA((3, max(rows, cols, 2))),
            pltpu.SemaphoreType.DMA((rows + cols,)),
        ],
        compiler_params=pltpu.CompilerParams(vmem_limit_bytes=LOCAL_BYTES),
        cost_estimate=COST,
        name="local_channels",
    )(onsite, psi.reshape(rows, cols, size, size), right, left)


def hop_kernel(base, count, first, last, capacity, *refs):
    refs = list(refs)
    take = lambda n: [refs.pop(0) for _ in range(n)]
    order, *terms = take(3)
    envs = take(2 if first else 1)
    acc_in = take(1 if first else 2)
    bufs = take(count)
    square = take(1)[0] if last else None
    acc = take(2)
    sums = take(1)[0]
    env = take(1)[0] if first else envs[0]
    psi, sems, env_sems = refs
    copies = [pltpu.make_async_copy(buf, psi.at[s], sems.at[s]) for s, buf in enumerate(bufs)]
    fills = [pltpu.make_async_copy(envs[e], env.at[e], env_sems.at[e]) for e in range(2)] if first else []
    for copy in copies + fills:
        copy.start()
    if first:
        copies.append(pltpu.make_async_copy(acc_in[0], acc[0], env_sems.at[2]))
        copies[-1].start()
        acc[1][...] = jnp.zeros(acc[1].shape, F32)
    else:
        for e in range(2):
            acc[e][...] = acc_in[e][...]
    for copy in copies:
        copy.wait()
    for fill in fills:
        fill.wait()

    def owner_step(s, carry):
        slot = order[base + s] * capacity
        words = [(e, terms[e][slot + r]) for e in range(2) for r in range(capacity)]
        mids = [dot(psi[s, w & 255], env[e, (w >> 16) & 255]).astype(BF16) for e, w in words]
        parts = [dot(env[e, w >> 24], mid) for (e, w), mid in zip(words, mids)]
        for (e, w), part in zip(words, parts):
            t = (w >> 8) & 255
            acc[e][t] = acc[e][t] + part
        return carry

    lax.fori_loop(0, count, owner_step, 0, unroll=2)
    if last:
        total = jnp.zeros(acc[0].shape[1:], F32)
        sec = acc[0].shape[0]
        first_psi = env.shape[1] - sec
        for e in range(2):
            total = lax.fori_loop(0, sec, lambda t, v, e=e: v + env[e, first_psi + t].astype(F32) * acc[e][t], total)
        lanes = lax.broadcasted_iota(jnp.int32, sums.shape, 1)
        sums[...] = jnp.where(lanes < sums.shape[1] // 2, jnp.sum(total), jnp.sum(square[...]))
    else:
        sums[...] = jnp.zeros(sums.shape, F32)


def hop_call(name, order, base, terms, envs, accs, bufs, last_args, owners, capacity):
    sec, size = accs[0].shape[:2]
    first, last = len(accs) == 1, bool(last_args)
    count = len(bufs)
    acc_shape = jax.ShapeDtypeStruct((sec, size, size), F32)
    out_shape = [acc_shape, acc_shape, jax.ShapeDtypeStruct((owners, size), F32) if last else TOKEN]
    if first:
        out_shape.append(jax.ShapeDtypeStruct((2,) + envs[0].shape, BF16))
    return pl.pallas_call(
        functools.partial(hop_kernel, base, count, first, last, capacity),
        out_shape=out_shape,
        in_specs=[SMEM] * 3
        + [ANY if first else VMEM] * (len(envs) + len(accs))
        + [ANY] * count
        + [VMEM] * len(last_args),
        out_specs=[VMEM] * len(out_shape),
        scratch_shapes=[
            pltpu.VMEM((count, sec, size, size), BF16),
            pltpu.SemaphoreType.DMA((count,)),
            pltpu.SemaphoreType.DMA((3,)),
        ],
        compiler_params=pltpu.CompilerParams(vmem_limit_bytes=VMEM_BYTES),
        cost_estimate=COST,
        name=name,
    )(order, *terms, *envs, *accs, *bufs, *last_args)


def hold_until(values, tokens):
    count = len(values)
    return pl.pallas_call(
        lambda *refs: None,
        out_shape=[jax.ShapeDtypeStruct(value.shape, value.dtype) for value in values],
        in_specs=[ANY] * (count + len(tokens)),
        out_specs=[ANY] * count,
        input_output_aliases={n: n for n in range(count)},
        compiler_params=pltpu.CompilerParams(vmem_limit_bytes=VMEM_BYTES),
        cost_estimate=COST,
        name="hold",
    )(*values, *tokens)


def finish_kernel(sums, psi, mine, theirs, applied, residual, quotient):
    lanes = lax.broadcasted_iota(jnp.int32, sums.shape, 1)
    half = sums.shape[1] // 2
    ratio = jnp.sum(jnp.where(lanes == 0, sums[...], 0.0)) / jnp.sum(jnp.where(lanes == half, sums[...], 0.0))
    quotient[0] = ratio
    for t in range(psi.shape[0]):
        hpsi = mine[t] + theirs[t]
        applied[t] = hpsi.astype(BF16)
        residual[t] = (hpsi - ratio * psi[t].astype(F32)).astype(BF16)


def finish_call(sums, psi, mine, theirs):
    shape = jax.ShapeDtypeStruct(psi.shape, BF16)
    return pl.pallas_call(
        finish_kernel,
        out_shape=(shape, shape, jax.ShapeDtypeStruct((1,), F32)),
        in_specs=[VMEM] * 4,
        out_specs=(VMEM, VMEM, SMEM),
        compiler_params=pltpu.CompilerParams(vmem_limit_bytes=VMEM_BYTES),
        name="finish",
    )(sums, psi, mine, theirs)


def term_words(source_device, source_block, cols, capacity):
    sec, hops = source_device.shape
    targets = source_device.reshape(-1)
    slots = targets * capacity + earlier_count(targets)
    index = jnp.arange(sec * hops, dtype=jnp.int32)
    t, k = index // hops, index % hops
    right, left = (t % cols) * hops + k, (cols + t // cols) * hops + k
    words = source_block.reshape(-1) | (t << 8) | (right << 16) | (left << 24)
    hit = slots[None, :] == index[:, None]
    return jnp.sum(jnp.where(hit, words[None, :], 0), axis=1)


def spread_everywhere(wavefunction, onsite_energy, left_env, right_env, source_device, source_block):
    owners = lax.axis_size("sector")
    sec = wavefunction.shape[0]
    hops = source_device.shape[1]
    capacity = sec * hops // owners
    core, x, y, z = 1, 2, 4, 8
    xy = x ^ y
    layers = owners // z

    def swap(value, mask):
        return lax.ppermute(value, "sector", [(i, i ^ mask) for i in range(owners)])

    def swap_middle(value):
        pairs = []
        for i in range(owners):
            layer = i // z
            pairs.append((i, (layers - 1 - layer) * z + i % z if layer in (1, 2) else i ^ core))
        return lax.ppermute(value, "sector", pairs)

    me = lax.axis_index("sector")
    outer = (me < z) | (me >= owners - z)
    layer_masks = [0, z, jnp.where(outer, 2 * z, 3 * z), jnp.where(outer, 3 * z, 2 * z)]
    groups = [
        [(0, 0), (0, x), (0, y), (1, 0)],
        [(0, xy), (1, y), (2, 0), (2, x), (2, y), (3, 0)],
        [(3, x), (3, y), (1, x)],
        [(2, xy), (3, xy), (1, xy)],
    ]
    order = jnp.stack([me ^ layer_masks[b] ^ bits for group in groups for b, bits in group])

    held = {(0, 0): wavefunction}
    state = {"base": 0}

    def hold(keys, *tokens):
        held.update(zip(keys, hold_until([held[key] for key in keys], tokens)))

    def run(group, last_args=()):
        out = hop_call(
            f"hops_{group}", order, state["base"], terms, state["envs"], state["accs"],
            tuple(held[key] for key in groups[group]), last_args, owners, capacity,
        )
        state["accs"] = out[:2]
        if group == 0:
            state["envs"] = out[3:]
        state["base"] += len(groups[group])
        return out[2]

    held[0, x], held[0, y] = swap(wavefunction, x), swap(wavefunction, y)
    held[1, 0] = swap(wavefunction, z)
    held["middle"] = swap_middle(wavefunction)
    terms = term_words(source_device, source_block, right_env.shape[0], capacity)
    terms = (terms, swap(terms, core))
    acc, square, held["env"] = local_call(onsite_energy, wavefunction, right_env, left_env, hops)
    hold([(0, x), (0, y), (1, 0), "middle", "env"], terms[1])

    held[0, xy] = swap(held[0, y], x)
    held[1, y] = swap(held[1, 0], y)
    held["outer"] = swap(held["middle"], z)
    held["middle_2"] = swap_middle(held[1, 0])
    held["env_sib"] = swap(held["env"], core)
    hold([(0, xy), (1, y), "outer", "middle_2", "env_sib"])

    held[2, 0] = jnp.where(outer, held["outer"], held["middle"])
    held[2, x], held[2, y] = swap(held[2, 0], x), swap(held[2, 0], y)
    held["outer_2"] = swap(held["middle_2"], z)
    state["accs"], state["envs"] = (acc,), (held["env"], held["env_sib"])
    done = run(0)
    hold([(2, x), (2, y), "outer_2", (0, x)], done)

    held[3, 0] = jnp.where(outer, held["outer_2"], held["middle_2"])
    held[3, x], held[3, y] = swap(held[3, 0], x), swap(held[3, 0], y)
    held[1, x] = swap(held[0, x], z)
    done = run(1)
    hold([(3, x), (3, y), (1, x), (2, y), (0, xy)], done)

    held[2, xy] = swap(held[2, y], x)
    held[3, xy] = swap(held[3, x], y)
    held[1, xy] = swap(held[0, xy], z)
    run(2)
    sums = run(3, (square,))
    sums = lax.all_to_all(sums, "sector", 0, 0, tiled=True)
    mine, theirs = state["accs"]
    return finish_call(sums, wavefunction, mine, swap(theirs, core))


def local(wavefunction, onsite_energy, left_env, right_env, source_device, source_block):
    owners = lax.axis_size("sector")
    sec, hops = source_device.shape
    fits = owners == 32 and sec <= 256 and (left_env.shape[0] + right_env.shape[0]) * hops <= 128
    fits = fits and (left_env.shape[1] - hops) % 2 == 0
    plan = spread_everywhere if fits and 2 * (sec * hops // owners) >= sec else ask_and_send
    return plan(wavefunction, onsite_energy, left_env, right_env, source_device, source_block)


def solution(mesh):
    return jax.shard_map(
        local,
        mesh=mesh,
        in_specs=(
            P(("groups", "sector"), None, None),
            P(("groups", "sector")),
            P(("groups", "sector"), None, None, None),
            P(("groups", "sector"), None, None, None),
            P(("groups", "sector"), None),
            P(("groups", "sector"), None),
        ),
        out_specs=(
            P(("groups", "sector"), None, None),
            P(("groups", "sector"), None, None),
            P("groups"),
        ),
        check_vma=False,
    )
```

```python
import functools

import jax
import jax.numpy as jnp
from jax import lax
from jax.experimental import pallas as pl
from jax.experimental.pallas import tpu as pltpu
from jax.sharding import PartitionSpec as P

F32 = jnp.float32
BF16 = jnp.bfloat16
VMEM_BYTES = 16 * 1024 * 1024
LOCAL_BYTES = 51 * 1024 * 1024
COST = pl.CostEstimate(flops=1, bytes_accessed=1, transcendentals=0)
ANY = pl.BlockSpec(memory_space=pl.ANY)
VMEM = pl.BlockSpec(memory_space=pltpu.VMEM)
HBM = pl.BlockSpec(memory_space=pltpu.HBM)
SMEM = pl.BlockSpec(memory_space=pltpu.SMEM)
TOKEN = jax.ShapeDtypeStruct((8, 128), F32)


def dot(a, b):
    return jnp.dot(a, b, preferred_element_type=F32)


def earlier_count(targets):
    length = targets.shape[0]
    row_iota = lax.broadcasted_iota(jnp.int32, (length, length), 0)
    col_iota = lax.broadcasted_iota(jnp.int32, (length, length), 1)
    earlier = (targets[:, None] == targets[None, :]) & (col_iota < row_iota)
    return jnp.sum(earlier.astype(jnp.int32), axis=1)


def ask_and_send(wavefunction, onsite_energy, left_env, right_env, source_device, source_block):
    owners = lax.axis_size("sector")
    sec_dev, block_size = wavefunction.shape[:2]
    left_count, channels = left_env.shape[:2]
    right_count = right_env.shape[0]
    hop_count = source_device.shape[1]
    local_count = channels - hop_count
    capacity = sec_dev * hop_count // owners
    targets = source_device.reshape(-1)
    slot_index = targets * capacity + earlier_count(targets)
    asked_for = jnp.zeros((owners * capacity,), jnp.int32).at[slot_index].set(source_block.reshape(-1))
    asked_for = lax.all_to_all(asked_for.reshape(owners, capacity), "sector", 0, 0, tiled=True)
    received = lax.all_to_all(wavefunction[asked_for], "sector", 0, 0, tiled=True)
    fetched = received.reshape(owners * capacity, block_size, block_size)[slot_index]
    fetched = fetched.reshape(left_count, right_count, hop_count, block_size, block_size)
    grid = wavefunction.reshape(left_count, right_count, 1, block_size, block_size)
    spread_out = jnp.broadcast_to(grid, (left_count, right_count, local_count, block_size, block_size))
    inputs_all = jnp.concatenate([spread_out, fetched], axis=2)
    middle = jnp.einsum("ijhab,jhbc->ijhac", inputs_all, right_env, preferred_element_type=F32).astype(BF16)
    summed = jnp.einsum("ihxa,ijhac->ijxc", left_env, middle, preferred_element_type=F32)
    psi_float = wavefunction.astype(F32)
    hpsi = summed.reshape(sec_dev, block_size, block_size) + onsite_energy[:, None, None] * psi_float
    numerator, denominator = lax.psum((jnp.sum(psi_float * hpsi), jnp.sum(psi_float * psi_float)), "sector")
    quotient = numerator / denominator
    residual = (hpsi - quotient * psi_float).astype(BF16)
    return hpsi.astype(BF16), residual, quotient.reshape(1)


def local_kernel(psi, right, left, acc, square, moved, psi_buf, r_buf, l_buf, middle, sems, moved_sems):
    rows, cols, size = psi.shape[0], psi.shape[1], psi.shape[2]
    chans = r_buf.shape[1]
    hops = right.shape[1] - chans
    psi_copy = pltpu.make_async_copy(psi, psi_buf, sems.at[0, 0])
    r_copy = [pltpu.make_async_copy(right.at[j, pl.ds(0, chans)], r_buf.at[j], sems.at[1, j]) for j in range(cols)]
    l_copy = [pltpu.make_async_copy(left.at[i, pl.ds(0, chans)], l_buf.at[i], sems.at[2, i]) for i in range(rows)]
    parts = [right.at[j, pl.ds(chans, hops)] for j in range(cols)] + [left.at[i, pl.ds(chans, hops)] for i in range(rows)]
    for n, part in enumerate(parts):
        parts[n] = pltpu.make_async_copy(part, moved.at[pl.ds(n * hops, hops)], moved_sems.at[n])
    for copy in [psi_copy] + r_copy + l_copy:
        copy.start()
    psi_copy.wait()
    for j in range(cols):
        r_copy[j].wait()
        if j == 1:
            for part in parts:
                part.start()
        column = psi_buf[:, j].reshape(rows * size, size)
        for h in range(0, chans, 2):
            pair = jnp.concatenate([r_buf[j, h], r_buf[j, h + 1]], axis=1)
            product = dot(column, pair).astype(BF16)
            for i in range(rows):
                for g in range(2):
                    block = product[i * size : (i + 1) * size, g * size : (g + 1) * size]
                    middle[i, pl.ds((h + g) * size, size), pl.ds(j * size, size)] = block
    total = jnp.zeros((size, size), F32)
    first = (rows + cols) * hops
    for i in range(rows):
        l_copy[i].wait()
        wide = jnp.concatenate([l_buf[i, h] for h in range(chans)], axis=1)
        summed = dot(wide, middle[i])
        for j in range(cols):
            moved[first + i * cols + j] = psi_buf[i, j]
            block = psi_buf[i, j].astype(F32)
            acc[i * cols + j] = summed[:, j * size : (j + 1) * size]
            total += block * block
    square[...] = total
    for part in parts:
        part.wait()


def local_call(psi, right, left, hops):
    sec, size = psi.shape[:2]
    rows, cols, chans = left.shape[0], right.shape[0], left.shape[1] - hops
    return pl.pallas_call(
        local_kernel,
        out_shape=(
            jax.ShapeDtypeStruct((sec, size, size), F32),
            jax.ShapeDtypeStruct((size, size), F32),
            jax.ShapeDtypeStruct(((rows + cols) * hops + sec, size, size), BF16),
        ),
        in_specs=[HBM] * 3,
        out_specs=[VMEM] * 3,
        scratch_shapes=[
            pltpu.VMEM((rows, cols, size, size), BF16),
            pltpu.VMEM((cols, chans, size, size), BF16),
            pltpu.VMEM((rows, chans, size, size), BF16),
            pltpu.VMEM((rows, chans * size, cols * size), BF16),
            pltpu.SemaphoreType.DMA((3, max(rows, cols, 2))),
            pltpu.SemaphoreType.DMA((rows + cols,)),
        ],
        compiler_params=pltpu.CompilerParams(vmem_limit_bytes=LOCAL_BYTES),
        cost_estimate=COST,
        name="local_channels",
    )(psi.reshape(rows, cols, size, size), right, left)


def hop_kernel(base, count, first, diagonal, last, capacity, *refs):
    refs = list(refs)
    take = lambda n: [refs.pop(0) for _ in range(n)]
    order, *terms = take(3)
    envs = take(2 if first else 1)
    acc_in = take(1 if first else 2)
    bufs = take(count)
    onsite = take(1)[0] if diagonal else None
    square = take(1)[0] if last else None
    acc = take(2)
    sums = take(1)[0]
    env = take(1)[0] if first else envs[0]
    (sems,) = refs
    fills = [pltpu.make_async_copy(envs[e], env.at[e], sems.at[e]) for e in range(2)] if first else []
    if first:
        fills.append(pltpu.make_async_copy(acc_in[0], acc[0], sems.at[2]))
        for fill in fills:
            fill.start()
        acc[1][...] = jnp.zeros(acc[1].shape, F32)
    else:
        for e in range(2):
            acc[e][...] = acc_in[e][...]
    for fill in fills:
        fill.wait()
    sec = acc[0].shape[0]
    first_psi = env.shape[1] - sec
    if diagonal:
        for t in range(sec):
            acc[0][t] = acc[0][t] + onsite[t] * env[0, first_psi + t].astype(F32)
    for s, psi in enumerate(bufs):
        slot = order[base + s] * capacity
        words = [(e, terms[e][slot + r]) for e in range(2) for r in range(capacity)]
        mids = [dot(psi[w & 255], env[e, (w >> 16) & 255]).astype(BF16) for e, w in words]
        parts = [dot(env[e, w >> 24], mid) for (e, w), mid in zip(words, mids)]
        for (e, w), part in zip(words, parts):
            t = (w >> 8) & 255
            acc[e][t] = acc[e][t] + part
    if last:
        total = jnp.zeros(acc[0].shape[1:], F32)
        for e in range(2):
            total = lax.fori_loop(0, sec, lambda t, v, e=e: v + env[e, first_psi + t].astype(F32) * acc[e][t], total)
        lanes = lax.broadcasted_iota(jnp.int32, sums.shape, 1)
        sums[...] = jnp.where(lanes < sums.shape[1] // 2, jnp.sum(total), jnp.sum(square[...]))
    else:
        sums[...] = jnp.zeros(sums.shape, F32)


def hop_call(name, order, base, terms, envs, accs, bufs, onsite, last_args, owners, capacity):
    sec, size = accs[0].shape[:2]
    first, last = len(accs) == 1, bool(last_args)
    count = len(bufs)
    acc_shape = jax.ShapeDtypeStruct((sec, size, size), F32)
    out_shape = [acc_shape, acc_shape, jax.ShapeDtypeStruct((owners, size), F32) if last else TOKEN]
    if first:
        out_shape.append(jax.ShapeDtypeStruct((2,) + envs[0].shape, BF16))
    return pl.pallas_call(
        functools.partial(hop_kernel, base, count, first, bool(onsite), last, capacity),
        out_shape=out_shape,
        in_specs=[SMEM] * 3
        + [ANY if first else VMEM] * (len(envs) + len(accs))
        + [VMEM] * count
        + [SMEM] * len(onsite)
        + [VMEM] * len(last_args),
        out_specs=[VMEM] * len(out_shape),
        scratch_shapes=[pltpu.SemaphoreType.DMA((3,))],
        compiler_params=pltpu.CompilerParams(vmem_limit_bytes=VMEM_BYTES),
        cost_estimate=COST,
        name=name,
    )(order, *terms, *envs, *accs, *bufs, *onsite, *last_args)


def hold_kernel(count, move, *refs):
    if move:
        src, dst = move
        flag, values, sem = refs[-count - 2], refs[: -count - 2], refs[-1]

        @pl.when(flag[0] != 0)
        def _():
            step = values[src].shape[0] // 4
            copies = []
            for n in range(4):
                part = pl.ds(n * step, step)
                copies.append(pltpu.make_async_copy(values[src].at[part], refs[dst - count - 1].at[part], sem.at[n]))
                copies[-1].start()
            for copy in copies:
                copy.wait()


def hold_until(values, tokens, move=None, flag=None):
    count = len(values)
    return pl.pallas_call(
        functools.partial(hold_kernel, count, move),
        out_shape=[jax.ShapeDtypeStruct(value.shape, value.dtype) for value in values],
        in_specs=[ANY] * (count + len(tokens)) + ([SMEM] if move else []),
        out_specs=[ANY] * count,
        scratch_shapes=[pltpu.SemaphoreType.DMA((4,))],
        input_output_aliases={n: n for n in range(count)},
        compiler_params=pltpu.CompilerParams(vmem_limit_bytes=VMEM_BYTES),
        cost_estimate=COST,
        name="hold",
    )(*values, *tokens, *([flag] if move else []))


def finish_kernel(sums, psi, mine, theirs, applied, residual, quotient):
    lanes = lax.broadcasted_iota(jnp.int32, sums.shape, 1)
    half = sums.shape[1] // 2
    ratio = jnp.sum(jnp.where(lanes == 0, sums[...], 0.0)) / jnp.sum(jnp.where(lanes == half, sums[...], 0.0))
    quotient[0] = ratio
    for t in range(psi.shape[0]):
        hpsi = mine[t] + theirs[t]
        applied[t] = hpsi.astype(BF16)
        residual[t] = (hpsi - ratio * psi[t].astype(F32)).astype(BF16)


def finish_call(sums, psi, mine, theirs):
    shape = jax.ShapeDtypeStruct(psi.shape, BF16)
    return pl.pallas_call(
        finish_kernel,
        out_shape=(shape, shape, jax.ShapeDtypeStruct((1,), F32)),
        in_specs=[VMEM] * 4,
        out_specs=(VMEM, VMEM, SMEM),
        compiler_params=pltpu.CompilerParams(vmem_limit_bytes=VMEM_BYTES),
        name="finish",
    )(sums, psi, mine, theirs)


def term_words(source_device, source_block, cols, capacity):
    sec, hops = source_device.shape
    targets = source_device.reshape(-1)
    slots = targets * capacity + earlier_count(targets)
    index = jnp.arange(sec * hops, dtype=jnp.int32)
    t, k = index // hops, index % hops
    right, left = (t % cols) * hops + k, (cols + t // cols) * hops + k
    words = source_block.reshape(-1) | (t << 8) | (right << 16) | (left << 24)
    hit = slots[None, :] == index[:, None]
    return jnp.sum(jnp.where(hit, words[None, :], 0), axis=1)


def spread_everywhere(wavefunction, onsite_energy, left_env, right_env, source_device, source_block):
    owners = lax.axis_size("sector")
    sec = wavefunction.shape[0]
    hops = source_device.shape[1]
    capacity = sec * hops // owners
    core, x, y, z = 1, 2, 4, 8
    xy = x ^ y
    layers = owners // z

    def swap(value, mask):
        return lax.ppermute(value, "sector", [(i, i ^ mask) for i in range(owners)])

    def swap_middle(value):
        pairs = []
        for i in range(owners):
            layer = i // z
            pairs.append((i, (layers - 1 - layer) * z + i % z if layer in (1, 2) else i ^ core))
        return lax.ppermute(value, "sector", pairs)

    me = lax.axis_index("sector")
    outer = ((me < z) | (me >= owners - z)).astype(jnp.int32).reshape(1)
    layer_masks = [0, z, 3 * z - outer * z, 2 * z + outer * z]
    groups = [
        [(0, 0), (0, x), (0, y), (1, 0), (0, xy), (1, y)],
        [(2, 0), (2, x), (2, y), (3, 0)],
        [(1, x), (3, y), (3, x)],
        [(1, xy), (3, xy), (2, xy)],
    ]
    order = jnp.concatenate([me ^ layer_masks[b] ^ jnp.full((1,), bits) for group in groups for b, bits in group])

    held = {(0, 0): wavefunction}
    state = {"base": 0}

    def hold(keys, *tokens, **move):
        held.update(zip(keys, hold_until([held[key] for key in keys], tokens, **move)))

    def run(group, onsite=(), last_args=()):
        out = hop_call(
            f"hops_{group}", order, state["base"], terms, state["envs"], state["accs"],
            tuple(held[key] for key in groups[group]), onsite, last_args, owners, capacity,
        )
        state["accs"] = out[:2]
        if group == 0:
            state["envs"] = out[3:]
        state["base"] += len(groups[group])
        return out[2]

    held[0, x], held[0, y] = swap(wavefunction, x), swap(wavefunction, y)
    held[1, 0] = swap(wavefunction, z)
    held["middle"] = swap_middle(wavefunction)
    terms = term_words(source_device, source_block, right_env.shape[0], capacity)
    terms = (terms, swap(terms, core))
    acc, square, held["env"] = local_call(wavefunction, right_env, left_env, hops)
    hold([(0, x), (0, y), "middle", (1, 0), "env"], terms[1])

    held[0, xy] = swap(held[0, y], x)
    held[1, y] = swap(held[1, 0], y)
    held["outer"] = swap(held["middle"], z)
    held["middle_2"] = swap_middle(held[1, 0])
    held["env_sib"] = swap(held["env"], core)
    hold(["env_sib", "middle", "middle_2", (1, y), (0, xy)], held["outer"], move=(5, 1), flag=outer)

    held[2, 0] = held["middle"]
    held[2, x], held[2, y] = swap(held[2, 0], x), swap(held[2, 0], y)
    held["outer_2"] = swap(held["middle_2"], z)
    state["accs"], state["envs"] = (acc,), (held["env"], held["env_sib"])
    done = run(0)
    hold(["middle_2", (0, x), (2, y), (2, x)], held["outer_2"], done, move=(4, 0), flag=outer)

    held[3, 0] = held["middle_2"]
    held[3, x], held[3, y] = swap(held[3, 0], x), swap(held[3, 0], y)
    held[1, x] = swap(held[0, x], z)
    done = run(1, (onsite_energy,))
    hold([(1, x), (2, y), (0, xy), (3, y), (3, x)], done)

    held[2, xy] = swap(held[2, y], x)
    held[3, xy] = swap(held[3, x], y)
    held[1, xy] = swap(held[0, xy], z)
    run(2)
    sums = run(3, (), (square,))
    sums = lax.all_to_all(sums, "sector", 0, 0, tiled=True)
    mine, theirs = state["accs"]
    return finish_call(sums, wavefunction, mine, swap(theirs, core))


def local(wavefunction, onsite_energy, left_env, right_env, source_device, source_block):
    owners = lax.axis_size("sector")
    sec, hops = source_device.shape
    fits = owners == 32 and sec <= 256 and (left_env.shape[0] + right_env.shape[0]) * hops <= 128
    fits = fits and (left_env.shape[1] - hops) % 2 == 0
    plan = spread_everywhere if fits and 2 * (sec * hops // owners) >= sec else ask_and_send
    return plan(wavefunction, onsite_energy, left_env, right_env, source_device, source_block)


def solution(mesh):
    return jax.shard_map(
        local,
        mesh=mesh,
        in_specs=(
            P(("groups", "sector"), None, None),
            P(("groups", "sector")),
            P(("groups", "sector"), None, None, None),
            P(("groups", "sector"), None, None, None),
            P(("groups", "sector"), None),
            P(("groups", "sector"), None),
        ),
        out_specs=(
            P(("groups", "sector"), None, None),
            P(("groups", "sector"), None, None),
            P("groups"),
        ),
        check_vma=False,
    )
```

```python
import functools

import jax
import jax.numpy as jnp
from jax import lax
from jax.experimental import pallas as pl
from jax.experimental.pallas import tpu as pltpu
from jax.sharding import PartitionSpec as P

F32 = jnp.float32
BF16 = jnp.bfloat16
VMEM_BYTES = 16 * 1024 * 1024
LOCAL_BYTES = 51 * 1024 * 1024
COST = pl.CostEstimate(flops=1, bytes_accessed=1, transcendentals=0)
ANY = pl.BlockSpec(memory_space=pl.ANY)
VMEM = pl.BlockSpec(memory_space=pltpu.VMEM)
HBM = pl.BlockSpec(memory_space=pltpu.HBM)
SMEM = pl.BlockSpec(memory_space=pltpu.SMEM)
TOKEN = jax.ShapeDtypeStruct((8, 128), F32)


def dot(a, b):
    return jnp.dot(a, b, preferred_element_type=F32)


def earlier_count(targets):
    length = targets.shape[0]
    row_iota = lax.broadcasted_iota(jnp.int32, (length, length), 0)
    col_iota = lax.broadcasted_iota(jnp.int32, (length, length), 1)
    earlier = (targets[:, None] == targets[None, :]) & (col_iota < row_iota)
    return jnp.sum(earlier.astype(jnp.int32), axis=1)


def ask_and_send(wavefunction, onsite_energy, left_env, right_env, source_device, source_block):
    owners = lax.axis_size("sector")
    sec_dev, block_size = wavefunction.shape[:2]
    left_count, channels = left_env.shape[:2]
    right_count = right_env.shape[0]
    hop_count = source_device.shape[1]
    local_count = channels - hop_count
    capacity = sec_dev * hop_count // owners
    targets = source_device.reshape(-1)
    slot_index = targets * capacity + earlier_count(targets)
    asked_for = jnp.zeros((owners * capacity,), jnp.int32).at[slot_index].set(source_block.reshape(-1))
    asked_for = lax.all_to_all(asked_for.reshape(owners, capacity), "sector", 0, 0, tiled=True)
    received = lax.all_to_all(wavefunction[asked_for], "sector", 0, 0, tiled=True)
    fetched = received.reshape(owners * capacity, block_size, block_size)[slot_index]
    fetched = fetched.reshape(left_count, right_count, hop_count, block_size, block_size)
    grid = wavefunction.reshape(left_count, right_count, 1, block_size, block_size)
    spread_out = jnp.broadcast_to(grid, (left_count, right_count, local_count, block_size, block_size))
    inputs_all = jnp.concatenate([spread_out, fetched], axis=2)
    middle = jnp.einsum("ijhab,jhbc->ijhac", inputs_all, right_env, preferred_element_type=F32).astype(BF16)
    summed = jnp.einsum("ihxa,ijhac->ijxc", left_env, middle, preferred_element_type=F32)
    psi_float = wavefunction.astype(F32)
    hpsi = summed.reshape(sec_dev, block_size, block_size) + onsite_energy[:, None, None] * psi_float
    numerator, denominator = lax.psum((jnp.sum(psi_float * hpsi), jnp.sum(psi_float * psi_float)), "sector")
    quotient = numerator / denominator
    residual = (hpsi - quotient * psi_float).astype(BF16)
    return hpsi.astype(BF16), residual, quotient.reshape(1)


def local_kernel(psi, right, left, acc, square, moved, psi_buf, r_buf, l_buf, middle, sems, moved_sems):
    rows, cols, size = psi.shape[0], psi.shape[1], psi.shape[2]
    chans = r_buf.shape[1]
    hops = right.shape[1] - chans
    psi_copy = pltpu.make_async_copy(psi, psi_buf, sems.at[0, 0])
    r_copy = [pltpu.make_async_copy(right.at[j, pl.ds(0, chans)], r_buf.at[j], sems.at[1, j]) for j in range(cols)]
    l_copy = [pltpu.make_async_copy(left.at[i, pl.ds(0, chans)], l_buf.at[i], sems.at[2, i]) for i in range(rows)]
    parts = [right.at[j, pl.ds(chans, hops)] for j in range(cols)] + [left.at[i, pl.ds(chans, hops)] for i in range(rows)]
    for n, part in enumerate(parts):
        parts[n] = pltpu.make_async_copy(part, moved.at[pl.ds(n * hops, hops)], moved_sems.at[n])
    for copy in [psi_copy] + r_copy + l_copy:
        copy.start()
    psi_copy.wait()
    for j in range(cols):
        r_copy[j].wait()
        if j == 1:
            for part in parts:
                part.start()
        column = psi_buf[:, j].reshape(rows * size, size)
        for h in range(0, chans, 2):
            pair = jnp.concatenate([r_buf[j, h], r_buf[j, h + 1]], axis=1)
            product = dot(column, pair).astype(BF16)
            for i in range(rows):
                for g in range(2):
                    block = product[i * size : (i + 1) * size, g * size : (g + 1) * size]
                    middle[i, pl.ds((h + g) * size, size), pl.ds(j * size, size)] = block
    total = jnp.zeros((size, size), F32)
    first = (rows + cols) * hops
    for i in range(rows):
        l_copy[i].wait()
        wide = jnp.concatenate([l_buf[i, h] for h in range(chans)], axis=1)
        summed = dot(wide, middle[i])
        for j in range(cols):
            moved[first + i * cols + j] = psi_buf[i, j]
            block = psi_buf[i, j].astype(F32)
            acc[i * cols + j] = summed[:, j * size : (j + 1) * size]
            total += block * block
    square[...] = total
    for part in parts:
        part.wait()


def local_call(psi, right, left, hops):
    sec, size = psi.shape[:2]
    rows, cols, chans = left.shape[0], right.shape[0], left.shape[1] - hops
    return pl.pallas_call(
        local_kernel,
        out_shape=(
            jax.ShapeDtypeStruct((sec, size, size), F32),
            jax.ShapeDtypeStruct((size, size), F32),
            jax.ShapeDtypeStruct(((rows + cols) * hops + sec, size, size), BF16),
        ),
        in_specs=[HBM] * 3,
        out_specs=[VMEM] * 3,
        scratch_shapes=[
            pltpu.VMEM((rows, cols, size, size), BF16),
            pltpu.VMEM((cols, chans, size, size), BF16),
            pltpu.VMEM((rows, chans, size, size), BF16),
            pltpu.VMEM((rows, chans * size, cols * size), BF16),
            pltpu.SemaphoreType.DMA((3, max(rows, cols, 2))),
            pltpu.SemaphoreType.DMA((rows + cols,)),
        ],
        compiler_params=pltpu.CompilerParams(vmem_limit_bytes=LOCAL_BYTES),
        cost_estimate=COST,
        name="local_channels",
    )(psi.reshape(rows, cols, size, size), right, left)


def hop_kernel(base, count, first, diagonal, tally, last, capacity, *refs):
    refs = list(refs)
    take = lambda n: [refs.pop(0) for _ in range(n)]
    order, *terms = take(3)
    envs = take(2 if first else 1)
    acc_in = take(1 if first else 2)
    bufs = take(count)
    onsite = take(1)[0] if diagonal else None
    tally_in = take(1)[0] if tally == "add" else None
    square = take(1)[0] if last else None
    acc = take(2)
    sums = take(1)[0]
    env = take(1)[0] if first else envs[0]
    (sems,) = refs
    fills = [pltpu.make_async_copy(envs[e], env.at[e], sems.at[e]) for e in range(2)] if first else []
    if first:
        fills.append(pltpu.make_async_copy(acc_in[0], acc[0], sems.at[2]))
        for fill in fills:
            fill.start()
        acc[1][...] = jnp.zeros(acc[1].shape, F32)
    else:
        for e in range(2):
            acc[e][...] = acc_in[e][...]
    for fill in fills:
        fill.wait()
    sec = acc[0].shape[0]
    first_psi = env.shape[1] - sec
    if diagonal:
        for t in range(sec):
            acc[0][t] = acc[0][t] + onsite[t] * env[0, first_psi + t].astype(F32)
    total = tally_in[...] if tally == "add" else jnp.zeros(acc[0].shape[1:], F32)
    for s, psi in enumerate(bufs):
        slot = order[base + s] * capacity
        words = [(e, terms[e][slot + r]) for e in range(2) for r in range(capacity)]
        mids = [dot(psi[w & 255], env[e, (w >> 16) & 255]).astype(BF16) for e, w in words]
        parts = [dot(env[e, w >> 24], mid) for (e, w), mid in zip(words, mids)]
        for (e, w), part in zip(words, parts):
            t = (w >> 8) & 255
            acc[e][t] = acc[e][t] + part
            if tally == "add":
                total += env[e, first_psi + t].astype(F32) * part
    if tally == "all":
        for e in range(2):
            total = lax.fori_loop(0, sec, lambda t, v, e=e: v + env[e, first_psi + t].astype(F32) * acc[e][t], total)
    if last:
        lanes = lax.broadcasted_iota(jnp.int32, sums.shape, 1)
        sums[...] = jnp.where(lanes < sums.shape[1] // 2, jnp.sum(total), jnp.sum(square[...]))
    elif tally:
        sums[...] = total
    else:
        sums[...] = jnp.zeros(sums.shape, F32)


def hop_call(name, order, base, terms, envs, accs, bufs, onsite, tally, tallies, square, owners, capacity):
    sec, size = accs[0].shape[:2]
    first, last = len(accs) == 1, bool(square)
    count = len(bufs)
    acc_shape = jax.ShapeDtypeStruct((sec, size, size), F32)
    side = (owners, size) if last else (size, size) if tally else (8, 128)
    out_shape = [acc_shape, acc_shape, jax.ShapeDtypeStruct(side, F32)]
    if first:
        out_shape.append(jax.ShapeDtypeStruct((2,) + envs[0].shape, BF16))
    return pl.pallas_call(
        functools.partial(hop_kernel, base, count, first, bool(onsite), tally, last, capacity),
        out_shape=out_shape,
        in_specs=[SMEM] * 3
        + [ANY if first else VMEM] * (len(envs) + len(accs))
        + [VMEM] * count
        + [SMEM] * len(onsite)
        + [VMEM] * len(tallies + square),
        out_specs=[VMEM] * len(out_shape),
        scratch_shapes=[pltpu.SemaphoreType.DMA((3,))],
        compiler_params=pltpu.CompilerParams(vmem_limit_bytes=VMEM_BYTES),
        cost_estimate=COST,
        name=name,
    )(order, *terms, *envs, *accs, *bufs, *onsite, *tallies, *square)


def hold_kernel(count, move, *refs):
    if move:
        src, dst = move
        flag, values, sem = refs[-count - 2], refs[: -count - 2], refs[-1]

        @pl.when(flag[0] != 0)
        def _():
            step = values[src].shape[0] // 4
            copies = []
            for n in range(4):
                part = pl.ds(n * step, step)
                copies.append(pltpu.make_async_copy(values[src].at[part], refs[dst - count - 1].at[part], sem.at[n]))
                copies[-1].start()
            for copy in copies:
                copy.wait()


def hold_until(values, tokens, move=None, flag=None):
    count = len(values)
    return pl.pallas_call(
        functools.partial(hold_kernel, count, move),
        out_shape=[jax.ShapeDtypeStruct(value.shape, value.dtype) for value in values],
        in_specs=[ANY] * (count + len(tokens)) + ([SMEM] if move else []),
        out_specs=[ANY] * count,
        scratch_shapes=[pltpu.SemaphoreType.DMA((4,))],
        input_output_aliases={n: n for n in range(count)},
        compiler_params=pltpu.CompilerParams(vmem_limit_bytes=VMEM_BYTES),
        cost_estimate=COST,
        name="hold",
    )(*values, *tokens, *([flag] if move else []))


def finish_kernel(sums, psi, mine, theirs, applied, residual, quotient):
    lanes = lax.broadcasted_iota(jnp.int32, sums.shape, 1)
    half = sums.shape[1] // 2
    ratio = jnp.sum(jnp.where(lanes == 0, sums[...], 0.0)) / jnp.sum(jnp.where(lanes == half, sums[...], 0.0))
    quotient[0] = ratio
    for t in range(psi.shape[0]):
        hpsi = mine[t] + theirs[t]
        applied[t] = hpsi.astype(BF16)
        residual[t] = (hpsi - ratio * psi[t].astype(F32)).astype(BF16)


def finish_call(sums, psi, mine, theirs):
    shape = jax.ShapeDtypeStruct(psi.shape, BF16)
    return pl.pallas_call(
        finish_kernel,
        out_shape=(shape, shape, jax.ShapeDtypeStruct((1,), F32)),
        in_specs=[VMEM] * 4,
        out_specs=(VMEM, VMEM, SMEM),
        compiler_params=pltpu.CompilerParams(vmem_limit_bytes=VMEM_BYTES),
        name="finish",
    )(sums, psi, mine, theirs)


def term_words(source_device, source_block, cols, capacity):
    sec, hops = source_device.shape
    targets = source_device.reshape(-1)
    slots = targets * capacity + earlier_count(targets)
    index = jnp.arange(sec * hops, dtype=jnp.int32)
    t, k = index // hops, index % hops
    right, left = (t % cols) * hops + k, (cols + t // cols) * hops + k
    words = source_block.reshape(-1) | (t << 8) | (right << 16) | (left << 24)
    hit = slots[None, :] == index[:, None]
    return jnp.sum(jnp.where(hit, words[None, :], 0), axis=1)


def spread_everywhere(wavefunction, onsite_energy, left_env, right_env, source_device, source_block):
    owners = lax.axis_size("sector")
    sec = wavefunction.shape[0]
    hops = source_device.shape[1]
    capacity = sec * hops // owners
    core, x, y, z = 1, 2, 4, 8
    xy = x ^ y
    layers = owners // z

    def swap(value, mask):
        return lax.ppermute(value, "sector", [(i, i ^ mask) for i in range(owners)])

    def swap_middle(value):
        pairs = []
        for i in range(owners):
            layer = i // z
            pairs.append((i, (layers - 1 - layer) * z + i % z if layer in (1, 2) else i ^ core))
        return lax.ppermute(value, "sector", pairs)

    me = lax.axis_index("sector")
    outer = ((me < z) | (me >= owners - z)).astype(jnp.int32).reshape(1)
    layer_masks = [0, z, 3 * z - outer * z, 2 * z + outer * z]
    groups = [
        [(0, 0), (0, x), (0, y), (1, 0), (0, xy), (1, y)],
        [(2, 0), (2, x), (2, y), (3, 0)],
        [(3, y), (3, x), (1, x)],
        [(1, xy), (2, xy), (3, xy)],
    ]
    order = jnp.concatenate([me ^ layer_masks[b] ^ jnp.full((1,), bits) for group in groups for b, bits in group])

    held = {(0, 0): wavefunction}
    state = {"base": 0}

    def hold(keys, *tokens, **move):
        held.update(zip(keys, hold_until([held[key] for key in keys], tokens, **move)))

    def run(group, onsite=(), tally=None, tallies=(), square=()):
        out = hop_call(
            f"hops_{group}", order, state["base"], terms, state["envs"], state["accs"],
            tuple(held[key] for key in groups[group]), onsite, tally, tallies, square, owners, capacity,
        )
        state["accs"] = out[:2]
        if group == 0:
            state["envs"] = out[3:]
        state["base"] += len(groups[group])
        return out[2]

    held[0, x], held[0, y] = swap(wavefunction, x), swap(wavefunction, y)
    held[1, 0] = swap(wavefunction, z)
    held["middle"] = swap_middle(wavefunction)
    terms = term_words(source_device, source_block, right_env.shape[0], capacity)
    terms = (terms, swap(terms, core))
    acc, square, held["env"] = local_call(wavefunction, right_env, left_env, hops)
    hold([(0, x), (0, y), "middle", (1, 0), "env"], terms[1])

    held[0, xy] = swap(held[0, y], x)
    held[1, y] = swap(held[1, 0], y)
    held["outer"] = swap(held["middle"], z)
    held["middle_2"] = swap_middle(held[1, 0])
    held["env_sib"] = swap(held["env"], core)
    hold(["env_sib", "middle", "middle_2", (1, y), (0, xy)], held["outer"], move=(5, 1), flag=outer)

    held[2, 0] = held["middle"]
    held[2, x], held[2, y] = swap(held[2, 0], x), swap(held[2, 0], y)
    held["outer_2"] = swap(held["middle_2"], z)
    state["accs"], state["envs"] = (acc,), (held["env"], held["env_sib"])
    done = run(0)
    hold(["middle_2", (0, x), (2, y), (2, x)], held["outer_2"], done, move=(4, 0), flag=outer)

    held[3, 0] = held["middle_2"]
    held[3, x], held[3, y] = swap(held[3, 0], x), swap(held[3, 0], y)
    held[1, x] = swap(held[0, x], z)
    done = run(1, (onsite_energy,))
    hold([(1, x), (2, y), (0, xy), (3, y), (3, x)], done)

    held[2, xy] = swap(held[2, y], x)
    held[3, xy] = swap(held[3, x], y)
    held[1, xy] = swap(held[0, xy], z)
    tally = run(2, (), "all")
    sums = run(3, (), "add", (tally,), (square,))
    sums = lax.all_to_all(sums, "sector", 0, 0, tiled=True)
    mine, theirs = state["accs"]
    return finish_call(sums, wavefunction, mine, swap(theirs, core))


def local(wavefunction, onsite_energy, left_env, right_env, source_device, source_block):
    owners = lax.axis_size("sector")
    sec, hops = source_device.shape
    fits = owners == 32 and sec <= 256 and (left_env.shape[0] + right_env.shape[0]) * hops <= 128
    fits = fits and (left_env.shape[1] - hops) % 2 == 0
    plan = spread_everywhere if fits and 2 * (sec * hops // owners) >= sec else ask_and_send
    return plan(wavefunction, onsite_energy, left_env, right_env, source_device, source_block)


def solution(mesh):
    return jax.shard_map(
        local,
        mesh=mesh,
        in_specs=(
            P(("groups", "sector"), None, None),
            P(("groups", "sector")),
            P(("groups", "sector"), None, None, None),
            P(("groups", "sector"), None, None, None),
            P(("groups", "sector"), None),
            P(("groups", "sector"), None),
        ),
        out_specs=(
            P(("groups", "sector"), None, None),
            P(("groups", "sector"), None, None),
            P("groups"),
        ),
        check_vma=False,
    )
```

```python
import functools

import jax
import jax.numpy as jnp
from jax import lax
from jax.experimental import pallas as pl
from jax.experimental.pallas import tpu as pltpu
from jax.sharding import PartitionSpec as P

F32 = jnp.float32
BF16 = jnp.bfloat16
VMEM_BYTES = 16 * 1024 * 1024
LOCAL_BYTES = 51 * 1024 * 1024
COST = pl.CostEstimate(flops=1, bytes_accessed=1, transcendentals=0)
ANY = pl.BlockSpec(memory_space=pl.ANY)
VMEM = pl.BlockSpec(memory_space=pltpu.VMEM)
HBM = pl.BlockSpec(memory_space=pltpu.HBM)
SMEM = pl.BlockSpec(memory_space=pltpu.SMEM)
TOKEN = jax.ShapeDtypeStruct((8, 128), F32)


def dot(a, b):
    return jnp.dot(a, b, preferred_element_type=F32)


def earlier_count(targets):
    length = targets.shape[0]
    row_iota = lax.broadcasted_iota(jnp.int32, (length, length), 0)
    col_iota = lax.broadcasted_iota(jnp.int32, (length, length), 1)
    earlier = (targets[:, None] == targets[None, :]) & (col_iota < row_iota)
    return jnp.sum(earlier.astype(jnp.int32), axis=1)


def ask_and_send(wavefunction, onsite_energy, left_env, right_env, source_device, source_block):
    owners = lax.axis_size("sector")
    sec_dev, block_size = wavefunction.shape[:2]
    left_count, channels = left_env.shape[:2]
    right_count = right_env.shape[0]
    hop_count = source_device.shape[1]
    local_count = channels - hop_count
    capacity = sec_dev * hop_count // owners
    targets = source_device.reshape(-1)
    slot_index = targets * capacity + earlier_count(targets)
    asked_for = jnp.zeros((owners * capacity,), jnp.int32).at[slot_index].set(source_block.reshape(-1))
    asked_for = lax.all_to_all(asked_for.reshape(owners, capacity), "sector", 0, 0, tiled=True)
    received = lax.all_to_all(wavefunction[asked_for], "sector", 0, 0, tiled=True)
    fetched = received.reshape(owners * capacity, block_size, block_size)[slot_index]
    fetched = fetched.reshape(left_count, right_count, hop_count, block_size, block_size)
    grid = wavefunction.reshape(left_count, right_count, 1, block_size, block_size)
    spread_out = jnp.broadcast_to(grid, (left_count, right_count, local_count, block_size, block_size))
    inputs_all = jnp.concatenate([spread_out, fetched], axis=2)
    middle = jnp.einsum("ijhab,jhbc->ijhac", inputs_all, right_env, preferred_element_type=F32).astype(BF16)
    summed = jnp.einsum("ihxa,ijhac->ijxc", left_env, middle, preferred_element_type=F32)
    psi_float = wavefunction.astype(F32)
    hpsi = summed.reshape(sec_dev, block_size, block_size) + onsite_energy[:, None, None] * psi_float
    numerator, denominator = lax.psum((jnp.sum(psi_float * hpsi), jnp.sum(psi_float * psi_float)), "sector")
    quotient = numerator / denominator
    residual = (hpsi - quotient * psi_float).astype(BF16)
    return hpsi.astype(BF16), residual, quotient.reshape(1)


def local_kernel(psi, right, left, acc, square, moved, psi_buf, r_buf, l_buf, middle, sems, moved_sems):
    rows, cols, size = psi.shape[0], psi.shape[1], psi.shape[2]
    chans = r_buf.shape[1]
    hops = right.shape[1] - chans
    psi_copy = pltpu.make_async_copy(psi, psi_buf, sems.at[0, 0])
    r_copy = [pltpu.make_async_copy(right.at[j, pl.ds(0, chans)], r_buf.at[j], sems.at[1, j]) for j in range(cols)]
    l_copy = [pltpu.make_async_copy(left.at[i, pl.ds(0, chans)], l_buf.at[i], sems.at[2, i]) for i in range(rows)]
    parts = [right.at[j, pl.ds(chans, hops)] for j in range(cols)] + [left.at[i, pl.ds(chans, hops)] for i in range(rows)]
    for n, part in enumerate(parts):
        parts[n] = pltpu.make_async_copy(part, moved.at[pl.ds(n * hops, hops)], moved_sems.at[n])
    for copy in [psi_copy] + r_copy + l_copy:
        copy.start()
    psi_copy.wait()
    for j in range(cols):
        r_copy[j].wait()
        if j == 1:
            for part in parts:
                part.start()
        column = psi_buf[:, j].reshape(rows * size, size)
        for h in range(0, chans, 2):
            pair = jnp.concatenate([r_buf[j, h], r_buf[j, h + 1]], axis=1)
            product = dot(column, pair).astype(BF16)
            for i in range(rows):
                for g in range(2):
                    block = product[i * size : (i + 1) * size, g * size : (g + 1) * size]
                    middle[i, pl.ds((h + g) * size, size), pl.ds(j * size, size)] = block
    total = jnp.zeros((size, size), F32)
    first = (rows + cols) * hops
    for i in range(rows):
        l_copy[i].wait()
        wide = jnp.concatenate([l_buf[i, h] for h in range(chans)], axis=1)
        summed = dot(wide, middle[i])
        for j in range(cols):
            moved[first + i * cols + j] = psi_buf[i, j]
            block = psi_buf[i, j].astype(F32)
            acc[i * cols + j] = summed[:, j * size : (j + 1) * size]
            total += block * block
    square[...] = total
    for part in parts:
        part.wait()


def local_call(psi, right, left, hops):
    sec, size = psi.shape[:2]
    rows, cols, chans = left.shape[0], right.shape[0], left.shape[1] - hops
    return pl.pallas_call(
        local_kernel,
        out_shape=(
            jax.ShapeDtypeStruct((sec, size, size), F32),
            jax.ShapeDtypeStruct((size, size), F32),
            jax.ShapeDtypeStruct(((rows + cols) * hops + sec, size, size), BF16),
        ),
        in_specs=[HBM] * 3,
        out_specs=[VMEM] * 3,
        scratch_shapes=[
            pltpu.VMEM((rows, cols, size, size), BF16),
            pltpu.VMEM((cols, chans, size, size), BF16),
            pltpu.VMEM((rows, chans, size, size), BF16),
            pltpu.VMEM((rows, chans * size, cols * size), BF16),
            pltpu.SemaphoreType.DMA((3, max(rows, cols, 2))),
            pltpu.SemaphoreType.DMA((rows + cols,)),
        ],
        compiler_params=pltpu.CompilerParams(vmem_limit_bytes=LOCAL_BYTES),
        cost_estimate=COST,
        name="local_channels",
    )(psi.reshape(rows, cols, size, size), right, left)


def hop_kernel(base, count, first, diagonal, tally, last, capacity, *refs):
    refs = list(refs)
    take = lambda n: [refs.pop(0) for _ in range(n)]
    order, *terms = take(3)
    envs = take(2 if first else 1)
    acc_in = take(1 if first else 2)
    bufs = take(count)
    onsite = take(1)[0] if diagonal else None
    tally_in = take(1)[0] if tally == "add" else None
    square = take(1)[0] if last else None
    acc = take(2)
    sums = take(1)[0]
    env = take(1)[0] if first else envs[0]
    (sems,) = refs
    fills = [pltpu.make_async_copy(envs[e], env.at[e], sems.at[e]) for e in range(2)] if first else []
    if first:
        fills.append(pltpu.make_async_copy(acc_in[0], acc[0], sems.at[2]))
        for fill in fills:
            fill.start()
        acc[1][...] = jnp.zeros(acc[1].shape, F32)
    else:
        for e in range(2):
            acc[e][...] = acc_in[e][...]
    for fill in fills:
        fill.wait()
    sec = acc[0].shape[0]
    first_psi = env.shape[1] - sec
    if diagonal:
        for t in range(sec):
            acc[0][t] = acc[0][t] + onsite[t] * env[0, first_psi + t].astype(F32)
    total = tally_in[...] if tally == "add" else jnp.zeros(acc[0].shape[1:], F32)
    for s, psi in enumerate(bufs):
        slot = order[base + s] * capacity
        words = [(e, terms[e][slot + r]) for e in range(2) for r in range(capacity)]
        mids = [dot(psi[w & 255], env[e, (w >> 16) & 255]).astype(BF16) for e, w in words]
        parts = [dot(env[e, w >> 24], mid) for (e, w), mid in zip(words, mids)]
        for (e, w), part in zip(words, parts):
            t = (w >> 8) & 255
            acc[e][t] = acc[e][t] + part
            if tally == "add":
                total += env[e, first_psi + t].astype(F32) * part
    if tally == "all":
        for e in range(2):
            total = lax.fori_loop(0, sec, lambda t, v, e=e: v + env[e, first_psi + t].astype(F32) * acc[e][t], total)
    if last:
        lanes = lax.broadcasted_iota(jnp.int32, sums.shape, 1)
        sums[...] = jnp.where(lanes < sums.shape[1] // 2, jnp.sum(total), jnp.sum(square[...]))
    elif tally:
        sums[...] = total
    else:
        sums[...] = jnp.zeros(sums.shape, F32)


def hop_call(name, order, base, terms, envs, accs, bufs, onsite, tally, tallies, square, owners, capacity):
    sec, size = accs[0].shape[:2]
    first, last = len(accs) == 1, bool(square)
    count = len(bufs)
    acc_shape = jax.ShapeDtypeStruct((sec, size, size), F32)
    side = (owners, size) if last else (size, size) if tally else (8, 128)
    out_shape = [acc_shape, acc_shape, jax.ShapeDtypeStruct(side, F32)]
    if first:
        out_shape.append(jax.ShapeDtypeStruct((2,) + envs[0].shape, BF16))
    return pl.pallas_call(
        functools.partial(hop_kernel, base, count, first, bool(onsite), tally, last, capacity),
        out_shape=out_shape,
        in_specs=[SMEM] * 3
        + [ANY if first else VMEM] * (len(envs) + len(accs))
        + [VMEM] * count
        + [SMEM] * len(onsite)
        + [VMEM] * len(tallies + square),
        out_specs=[VMEM] * len(out_shape),
        scratch_shapes=[pltpu.SemaphoreType.DMA((3,))],
        compiler_params=pltpu.CompilerParams(vmem_limit_bytes=VMEM_BYTES),
        cost_estimate=COST,
        name=name,
    )(order, *terms, *envs, *accs, *bufs, *onsite, *tallies, *square)


def hold_kernel(count, move, *refs):
    if move:
        src, dst = move
        flag, values, sem = refs[-count - 2], refs[: -count - 2], refs[-1]

        @pl.when(flag[0] != 0)
        def _():
            step = values[src].shape[0] // 4
            copies = []
            for n in range(4):
                part = pl.ds(n * step, step)
                copies.append(pltpu.make_async_copy(values[src].at[part], refs[dst - count - 1].at[part], sem.at[n]))
                copies[-1].start()
            for copy in copies:
                copy.wait()


def hold_until(values, tokens, move=None, flag=None):
    count = len(values)
    return pl.pallas_call(
        functools.partial(hold_kernel, count, move),
        out_shape=[jax.ShapeDtypeStruct(value.shape, value.dtype) for value in values],
        in_specs=[ANY] * (count + len(tokens)) + ([SMEM] if move else []),
        out_specs=[ANY] * count,
        scratch_shapes=[pltpu.SemaphoreType.DMA((4,))],
        input_output_aliases={n: n for n in range(count)},
        compiler_params=pltpu.CompilerParams(vmem_limit_bytes=VMEM_BYTES),
        cost_estimate=COST,
        name="hold",
    )(*values, *tokens, *([flag] if move else []))


def finish_kernel(sums, psi, mine, theirs, applied, residual, quotient):
    lanes = lax.broadcasted_iota(jnp.int32, sums.shape, 1)
    half = sums.shape[1] // 2
    ratio = jnp.sum(jnp.where(lanes == 0, sums[...], 0.0)) / jnp.sum(jnp.where(lanes == half, sums[...], 0.0))
    quotient[0] = ratio
    for t in range(psi.shape[0]):
        hpsi = mine[t] + theirs[t]
        applied[t] = hpsi.astype(BF16)
        residual[t] = (hpsi - ratio * psi[t].astype(F32)).astype(BF16)


def finish_call(sums, psi, mine, theirs):
    shape = jax.ShapeDtypeStruct(psi.shape, BF16)
    return pl.pallas_call(
        finish_kernel,
        out_shape=(shape, shape, jax.ShapeDtypeStruct((1,), F32)),
        in_specs=[VMEM] * 4,
        out_specs=(VMEM, VMEM, SMEM),
        compiler_params=pltpu.CompilerParams(vmem_limit_bytes=VMEM_BYTES),
        name="finish",
    )(sums, psi, mine, theirs)


def term_words(source_device, source_block, cols, capacity):
    sec, hops = source_device.shape
    targets = source_device.reshape(-1)
    slots = targets * capacity + earlier_count(targets)
    index = jnp.arange(sec * hops, dtype=jnp.int32)
    t, k = index // hops, index % hops
    right, left = (t % cols) * hops + k, (cols + t // cols) * hops + k
    words = source_block.reshape(-1) | (t << 8) | (right << 16) | (left << 24)
    hit = slots[None, :] == index[:, None]
    return jnp.sum(jnp.where(hit, words[None, :], 0), axis=1)


def spread_everywhere(wavefunction, onsite_energy, left_env, right_env, source_device, source_block):
    owners = lax.axis_size("sector")
    sec = wavefunction.shape[0]
    hops = source_device.shape[1]
    capacity = sec * hops // owners
    core, x, y, z = 1, 2, 4, 8
    xy = x ^ y
    layers = owners // z

    def swap(value, mask):
        return lax.ppermute(value, "sector", [(i, i ^ mask) for i in range(owners)])

    def swap_middle(value):
        pairs = []
        for i in range(owners):
            layer = i // z
            pairs.append((i, (layers - 1 - layer) * z + i % z if layer in (1, 2) else i ^ core))
        return lax.ppermute(value, "sector", pairs)

    me = lax.axis_index("sector")
    outer = ((me < z) | (me >= owners - z)).astype(jnp.int32).reshape(1)
    layer_masks = [0, z, 3 * z - outer * z, 2 * z + outer * z]
    groups = [
        [(0, 0), (0, x), (0, y), (1, 0), (0, xy), (1, y)],
        [(2, 0), (2, x), (2, y), (3, 0)],
        [(3, y), (3, x), (1, x)],
        [(1, xy), (2, xy), (3, xy)],
    ]
    order = jnp.concatenate([me ^ layer_masks[b] ^ jnp.full((1,), bits) for group in groups for b, bits in group])

    held = {(0, 0): wavefunction}
    state = {"base": 0}

    def hold(keys, *tokens, **move):
        held.update(zip(keys, hold_until([held[key] for key in keys], tokens, **move)))

    def run(group, onsite=(), tally=None, tallies=(), square=()):
        out = hop_call(
            f"hops_{group}", order, state["base"], terms, state["envs"], state["accs"],
            tuple(held[key] for key in groups[group]), onsite, tally, tallies, square, owners, capacity,
        )
        state["accs"] = out[:2]
        if group == 0:
            state["envs"] = out[3:]
        state["base"] += len(groups[group])
        return out[2]

    held[0, x], held[0, y] = swap(wavefunction, x), swap(wavefunction, y)
    held[1, 0] = swap(wavefunction, z)
    held["middle"] = swap_middle(wavefunction)
    terms = term_words(source_device, source_block, right_env.shape[0], capacity)
    terms = (terms, swap(terms, core))
    acc, square, held["env"] = local_call(wavefunction, right_env, left_env, hops)
    hold([(0, x), (0, y), "middle", (1, 0), "env"], terms[1])

    held[0, xy] = swap(held[0, y], x)
    held[1, y] = swap(held[1, 0], y)
    held["outer"] = swap(held["middle"], z)
    held["middle_2"] = swap_middle(held[1, 0])
    held["env_sib"] = swap(held["env"], core)
    hold(["middle"], held["outer"], move=(1, 0), flag=outer)
    hold(["env_sib", "middle", "middle_2", (1, y), (0, xy)])

    held[2, 0] = held["middle"]
    held[2, x], held[2, y] = swap(held[2, 0], x), swap(held[2, 0], y)
    held["outer_2"] = swap(held["middle_2"], z)
    state["accs"], state["envs"] = (acc,), (held["env"], held["env_sib"])
    done = run(0)
    hold(["middle_2", (0, x), (2, y), (2, x)], held["outer_2"], done, move=(4, 0), flag=outer)

    held[3, 0] = held["middle_2"]
    held[3, x], held[3, y] = swap(held[3, 0], x), swap(held[3, 0], y)
    held[1, x] = swap(held[0, x], z)
    done = run(1, (onsite_energy,))
    hold([(1, x), (2, y), (0, xy), (3, y), (3, x)], done)

    held[2, xy] = swap(held[2, y], x)
    held[3, xy] = swap(held[3, x], y)
    held[1, xy] = swap(held[0, xy], z)
    tally = run(2, (), "all")
    sums = run(3, (), "add", (tally,), (square,))
    sums = lax.all_to_all(sums, "sector", 0, 0, tiled=True)
    mine, theirs = state["accs"]
    return finish_call(sums, wavefunction, mine, swap(theirs, core))


def local(wavefunction, onsite_energy, left_env, right_env, source_device, source_block):
    owners = lax.axis_size("sector")
    sec, hops = source_device.shape
    fits = owners == 32 and sec <= 256 and (left_env.shape[0] + right_env.shape[0]) * hops <= 128
    fits = fits and (left_env.shape[1] - hops) % 2 == 0
    plan = spread_everywhere if fits and 2 * (sec * hops // owners) >= sec else ask_and_send
    return plan(wavefunction, onsite_energy, left_env, right_env, source_device, source_block)


def solution(mesh):
    return jax.shard_map(
        local,
        mesh=mesh,
        in_specs=(
            P(("groups", "sector"), None, None),
            P(("groups", "sector")),
            P(("groups", "sector"), None, None, None),
            P(("groups", "sector"), None, None, None),
            P(("groups", "sector"), None),
            P(("groups", "sector"), None),
        ),
        out_specs=(
            P(("groups", "sector"), None, None),
            P(("groups", "sector"), None, None),
            P("groups"),
        ),
        check_vma=False,
    )
```

```python
import functools

import jax
import jax.numpy as jnp
from jax import lax
from jax.experimental import pallas as pl
from jax.experimental.pallas import tpu as pltpu
from jax.sharding import PartitionSpec as P

F32 = jnp.float32
BF16 = jnp.bfloat16
VMEM_BYTES = 16 * 1024 * 1024
LOCAL_BYTES = 51 * 1024 * 1024
COST = pl.CostEstimate(flops=1, bytes_accessed=1, transcendentals=0)
ANY = pl.BlockSpec(memory_space=pl.ANY)
VMEM = pl.BlockSpec(memory_space=pltpu.VMEM)
HBM = pl.BlockSpec(memory_space=pltpu.HBM)
SMEM = pl.BlockSpec(memory_space=pltpu.SMEM)
TOKEN = jax.ShapeDtypeStruct((8, 128), F32)


def dot(a, b):
    return jnp.dot(a, b, preferred_element_type=F32)


def earlier_count(targets):
    length = targets.shape[0]
    row_iota = lax.broadcasted_iota(jnp.int32, (length, length), 0)
    col_iota = lax.broadcasted_iota(jnp.int32, (length, length), 1)
    earlier = (targets[:, None] == targets[None, :]) & (col_iota < row_iota)
    return jnp.sum(earlier.astype(jnp.int32), axis=1)


def ask_and_send(wavefunction, onsite_energy, left_env, right_env, source_device, source_block):
    owners = lax.axis_size("sector")
    sec_dev, block_size = wavefunction.shape[:2]
    left_count, channels = left_env.shape[:2]
    right_count = right_env.shape[0]
    hop_count = source_device.shape[1]
    local_count = channels - hop_count
    capacity = sec_dev * hop_count // owners
    targets = source_device.reshape(-1)
    slot_index = targets * capacity + earlier_count(targets)
    asked_for = jnp.zeros((owners * capacity,), jnp.int32).at[slot_index].set(source_block.reshape(-1))
    asked_for = lax.all_to_all(asked_for.reshape(owners, capacity), "sector", 0, 0, tiled=True)
    received = lax.all_to_all(wavefunction[asked_for], "sector", 0, 0, tiled=True)
    fetched = received.reshape(owners * capacity, block_size, block_size)[slot_index]
    fetched = fetched.reshape(left_count, right_count, hop_count, block_size, block_size)
    grid = wavefunction.reshape(left_count, right_count, 1, block_size, block_size)
    spread_out = jnp.broadcast_to(grid, (left_count, right_count, local_count, block_size, block_size))
    inputs_all = jnp.concatenate([spread_out, fetched], axis=2)
    middle = jnp.einsum("ijhab,jhbc->ijhac", inputs_all, right_env, preferred_element_type=F32).astype(BF16)
    summed = jnp.einsum("ihxa,ijhac->ijxc", left_env, middle, preferred_element_type=F32)
    psi_float = wavefunction.astype(F32)
    hpsi = summed.reshape(sec_dev, block_size, block_size) + onsite_energy[:, None, None] * psi_float
    numerator, denominator = lax.psum((jnp.sum(psi_float * hpsi), jnp.sum(psi_float * psi_float)), "sector")
    quotient = numerator / denominator
    residual = (hpsi - quotient * psi_float).astype(BF16)
    return hpsi.astype(BF16), residual, quotient.reshape(1)


def local_kernel(psi, right, left, acc, square, moved, psi_buf, r_buf, l_buf, middle, sems, moved_sems):
    rows, cols, size = psi.shape[0], psi.shape[1], psi.shape[2]
    chans = r_buf.shape[1]
    hops = right.shape[1] - chans
    psi_copy = pltpu.make_async_copy(psi, psi_buf, sems.at[0, 0])
    r_copy = [pltpu.make_async_copy(right.at[j, pl.ds(0, chans)], r_buf.at[j], sems.at[1, j]) for j in range(cols)]
    l_copy = [pltpu.make_async_copy(left.at[i, pl.ds(0, chans)], l_buf.at[i], sems.at[2, i]) for i in range(rows)]
    parts = [right.at[j, pl.ds(chans, hops)] for j in range(cols)] + [left.at[i, pl.ds(chans, hops)] for i in range(rows)]
    for n, part in enumerate(parts):
        parts[n] = pltpu.make_async_copy(part, moved.at[pl.ds(n * hops, hops)], moved_sems.at[n])
    for copy in [psi_copy] + r_copy + l_copy:
        copy.start()
    psi_copy.wait()
    for j in range(cols):
        r_copy[j].wait()
        if j == 1:
            for part in parts:
                part.start()
        column = psi_buf[:, j].reshape(rows * size, size)
        for h in range(0, chans, 2):
            pair = jnp.concatenate([r_buf[j, h], r_buf[j, h + 1]], axis=1)
            product = dot(column, pair).astype(BF16)
            for i in range(rows):
                for g in range(2):
                    block = product[i * size : (i + 1) * size, g * size : (g + 1) * size]
                    middle[i, pl.ds((h + g) * size, size), pl.ds(j * size, size)] = block
    total = jnp.zeros((size, size), F32)
    first = (rows + cols) * hops
    for i in range(rows):
        l_copy[i].wait()
        wide = jnp.concatenate([l_buf[i, h] for h in range(chans)], axis=1)
        summed = dot(wide, middle[i])
        for j in range(cols):
            moved[first + i * cols + j] = psi_buf[i, j]
            block = psi_buf[i, j].astype(F32)
            acc[i * cols + j] = summed[:, j * size : (j + 1) * size]
            total += block * block
    square[...] = total
    for part in parts:
        part.wait()


def local_call(psi, right, left, hops):
    sec, size = psi.shape[:2]
    rows, cols, chans = left.shape[0], right.shape[0], left.shape[1] - hops
    return pl.pallas_call(
        local_kernel,
        out_shape=(
            jax.ShapeDtypeStruct((sec, size, size), F32),
            jax.ShapeDtypeStruct((size, size), F32),
            jax.ShapeDtypeStruct(((rows + cols) * hops + sec, size, size), BF16),
        ),
        in_specs=[HBM] * 3,
        out_specs=[VMEM] * 3,
        scratch_shapes=[
            pltpu.VMEM((rows, cols, size, size), BF16),
            pltpu.VMEM((cols, chans, size, size), BF16),
            pltpu.VMEM((rows, chans, size, size), BF16),
            pltpu.VMEM((rows, chans * size, cols * size), BF16),
            pltpu.SemaphoreType.DMA((3, max(rows, cols, 2))),
            pltpu.SemaphoreType.DMA((rows + cols,)),
        ],
        compiler_params=pltpu.CompilerParams(vmem_limit_bytes=LOCAL_BYTES),
        cost_estimate=COST,
        name="local_channels",
    )(psi.reshape(rows, cols, size, size), right, left)


def hop_kernel(base, count, first, diagonal, tally, last, capacity, *refs):
    refs = list(refs)
    take = lambda n: [refs.pop(0) for _ in range(n)]
    order, *terms = take(3)
    envs = take(2 if first else 1)
    acc_in = take(1 if first else 2)
    bufs = take(count)
    onsite = take(1)[0] if diagonal else None
    tally_in = take(1)[0] if tally == "add" else None
    square = take(1)[0] if last else None
    acc = take(2)
    sums = take(1)[0]
    env = take(1)[0] if first else envs[0]
    (sems,) = refs
    fills = [pltpu.make_async_copy(envs[e], env.at[e], sems.at[e]) for e in range(2)] if first else []
    if first:
        fills.append(pltpu.make_async_copy(acc_in[0], acc[0], sems.at[2]))
        for fill in fills:
            fill.start()
        acc[1][...] = jnp.zeros(acc[1].shape, F32)
    else:
        for e in range(2):
            acc[e][...] = acc_in[e][...]
    for fill in fills:
        fill.wait()
    sec = acc[0].shape[0]
    first_psi = env.shape[1] - sec
    if diagonal:
        for t in range(sec):
            acc[0][t] = acc[0][t] + onsite[t] * env[0, first_psi + t].astype(F32)
    total = tally_in[...] if tally == "add" else jnp.zeros(acc[0].shape[1:], F32)
    for s, psi in enumerate(bufs):
        slot = order[base + s] * capacity
        words = [(e, terms[e][slot + r]) for e in range(2) for r in range(capacity)]
        mids = [dot(psi[w & 255], env[e, (w >> 16) & 255]).astype(BF16) for e, w in words]
        parts = [dot(env[e, w >> 24], mid) for (e, w), mid in zip(words, mids)]
        for (e, w), part in zip(words, parts):
            t = (w >> 8) & 255
            acc[e][t] = acc[e][t] + part
            if tally == "add":
                total += env[e, first_psi + t].astype(F32) * part
    if tally == "all":
        for e in range(2):
            total = lax.fori_loop(0, sec, lambda t, v, e=e: v + env[e, first_psi + t].astype(F32) * acc[e][t], total)
    if last:
        lanes = lax.broadcasted_iota(jnp.int32, sums.shape, 1)
        sums[...] = jnp.where(lanes < sums.shape[1] // 2, jnp.sum(total), jnp.sum(square[...]))
    elif tally:
        sums[...] = total
    else:
        sums[...] = jnp.zeros(sums.shape, F32)


def hop_call(name, order, base, terms, envs, accs, bufs, onsite, tally, tallies, square, owners, capacity):
    sec, size = accs[0].shape[:2]
    first, last = len(accs) == 1, bool(square)
    count = len(bufs)
    acc_shape = jax.ShapeDtypeStruct((sec, size, size), F32)
    side = (owners, size) if last else (size, size) if tally else (8, 128)
    out_shape = [acc_shape, acc_shape, jax.ShapeDtypeStruct(side, F32)]
    if first:
        out_shape.append(jax.ShapeDtypeStruct((2,) + envs[0].shape, BF16))
    return pl.pallas_call(
        functools.partial(hop_kernel, base, count, first, bool(onsite), tally, last, capacity),
        out_shape=out_shape,
        in_specs=[SMEM] * 3
        + [ANY if first else VMEM] * (len(envs) + len(accs))
        + [VMEM] * count
        + [SMEM] * len(onsite)
        + [VMEM] * len(tallies + square),
        out_specs=[VMEM] * len(out_shape),
        scratch_shapes=[pltpu.SemaphoreType.DMA((3,))],
        compiler_params=pltpu.CompilerParams(vmem_limit_bytes=VMEM_BYTES),
        cost_estimate=COST,
        name=name,
    )(order, *terms, *envs, *accs, *bufs, *onsite, *tallies, *square)


def hold_kernel(count, move, *refs):
    if move:
        src, dst = move
        flag, values, sem = refs[-count - 2], refs[: -count - 2], refs[-1]

        @pl.when(flag[0] != 0)
        def _():
            step = values[src].shape[0] // 4
            copies = []
            for n in range(4):
                part = pl.ds(n * step, step)
                copies.append(pltpu.make_async_copy(values[src].at[part], refs[dst - count - 1].at[part], sem.at[n]))
                copies[-1].start()
            for copy in copies:
                copy.wait()


def hold_until(values, tokens, move=None, flag=None):
    count = len(values)
    return pl.pallas_call(
        functools.partial(hold_kernel, count, move),
        out_shape=[jax.ShapeDtypeStruct(value.shape, value.dtype) for value in values],
        in_specs=[ANY] * (count + len(tokens)) + ([SMEM] if move else []),
        out_specs=[ANY] * count,
        scratch_shapes=[pltpu.SemaphoreType.DMA((4,))],
        input_output_aliases={n: n for n in range(count)},
        compiler_params=pltpu.CompilerParams(vmem_limit_bytes=VMEM_BYTES),
        cost_estimate=COST,
        name="hold",
    )(*values, *tokens, *([flag] if move else []))


def finish_kernel(sums, psi, mine, theirs, applied, residual, quotient):
    lanes = lax.broadcasted_iota(jnp.int32, sums.shape, 1)
    half = sums.shape[1] // 2
    ratio = jnp.sum(jnp.where(lanes == 0, sums[...], 0.0)) / jnp.sum(jnp.where(lanes == half, sums[...], 0.0))
    quotient[0] = ratio
    for t in range(psi.shape[0]):
        hpsi = mine[t] + theirs[t]
        applied[t] = hpsi.astype(BF16)
        residual[t] = (hpsi - ratio * psi[t].astype(F32)).astype(BF16)


def finish_call(sums, psi, mine, theirs):
    shape = jax.ShapeDtypeStruct(psi.shape, BF16)
    return pl.pallas_call(
        finish_kernel,
        out_shape=(shape, shape, jax.ShapeDtypeStruct((1,), F32)),
        in_specs=[VMEM] * 4,
        out_specs=(VMEM, VMEM, SMEM),
        compiler_params=pltpu.CompilerParams(vmem_limit_bytes=VMEM_BYTES),
        name="finish",
    )(sums, psi, mine, theirs)


def term_words(source_device, source_block, cols, capacity):
    sec, hops = source_device.shape
    targets = source_device.reshape(-1)
    slots = targets * capacity + earlier_count(targets)
    index = jnp.arange(sec * hops, dtype=jnp.int32)
    t, k = index // hops, index % hops
    right, left = (t % cols) * hops + k, (cols + t // cols) * hops + k
    words = source_block.reshape(-1) | (t << 8) | (right << 16) | (left << 24)
    hit = slots[None, :] == index[:, None]
    return jnp.sum(jnp.where(hit, words[None, :], 0), axis=1)


def spread_everywhere(wavefunction, onsite_energy, left_env, right_env, source_device, source_block):
    owners = lax.axis_size("sector")
    sec = wavefunction.shape[0]
    hops = source_device.shape[1]
    capacity = sec * hops // owners
    core, x, y, z = 1, 2, 4, 8
    xy = x ^ y
    layers = owners // z

    def swap(value, mask):
        return lax.ppermute(value, "sector", [(i, i ^ mask) for i in range(owners)])

    def swap_middle(value):
        pairs = []
        for i in range(owners):
            layer = i // z
            pairs.append((i, (layers - 1 - layer) * z + i % z if layer in (1, 2) else i ^ core))
        return lax.ppermute(value, "sector", pairs)

    me = lax.axis_index("sector")
    outer = ((me < z) | (me >= owners - z)).astype(jnp.int32).reshape(1)
    layer_masks = [0, z, 3 * z - outer * z, 2 * z + outer * z]
    groups = [
        [(0, 0), (0, x), (0, y), (1, 0), (0, xy), (1, y)],
        [(2, 0), (2, x), (2, y), (3, 0)],
        [(3, y), (3, x), (1, x)],
        [(3, xy), (2, xy), (1, xy)],
    ]
    order = jnp.concatenate([me ^ layer_masks[b] ^ jnp.full((1,), bits) for group in groups for b, bits in group])

    held = {(0, 0): wavefunction}
    state = {"base": 0}

    def hold(keys, *tokens, **move):
        held.update(zip(keys, hold_until([held[key] for key in keys], tokens, **move)))

    def run(group, onsite=(), tally=None, tallies=(), square=()):
        out = hop_call(
            f"hops_{group}", order, state["base"], terms, state["envs"], state["accs"],
            tuple(held[key] for key in groups[group]), onsite, tally, tallies, square, owners, capacity,
        )
        state["accs"] = out[:2]
        if group == 0:
            state["envs"] = out[3:]
        state["base"] += len(groups[group])
        return out[2]

    held[0, x], held[0, y] = swap(wavefunction, x), swap(wavefunction, y)
    held[1, 0] = swap(wavefunction, z)
    held["middle"] = swap_middle(wavefunction)
    terms = term_words(source_device, source_block, right_env.shape[0], capacity)
    terms = (terms, swap(terms, core))
    acc, square, held["env"] = local_call(wavefunction, right_env, left_env, hops)
    hold([(0, x), (0, y), "middle", (1, 0), "env"], terms[1])

    held[0, xy] = swap(held[0, y], x)
    held[1, y] = swap(held[1, 0], y)
    held["outer"] = swap(held["middle"], z)
    held["middle_2"] = swap_middle(held[1, 0])
    held["env_sib"] = swap(held["env"], core)
    hold(["middle"], held["outer"], move=(1, 0), flag=outer)
    hold(["env_sib", "middle_2", (1, y), (0, xy), "middle"])

    held[2, 0] = held["middle"]
    held[2, x], held[2, y] = swap(held[2, 0], x), swap(held[2, 0], y)
    held["outer_2"] = swap(held["middle_2"], z)
    state["accs"], state["envs"] = (acc,), (held["env"], held["env_sib"])
    done = run(0)
    hold(["middle_2", (0, x), (2, y), (2, x)], held["outer_2"], done, move=(4, 0), flag=outer)

    held[3, 0] = held["middle_2"]
    held[3, x], held[3, y] = swap(held[3, 0], x), swap(held[3, 0], y)
    held[1, x] = swap(held[0, x], z)
    done = run(1, (onsite_energy,))
    hold([(1, x), (2, y), (0, xy), (3, y), (3, x)], done)

    held[2, xy] = swap(held[2, y], x)
    held[3, xy] = swap(held[3, x], y)
    held[1, xy] = swap(held[0, xy], z)
    tally = run(2, (), "all")
    sums = run(3, (), "add", (tally,), (square,))
    sums = lax.all_to_all(sums, "sector", 0, 0, tiled=True)
    mine, theirs = state["accs"]
    return finish_call(sums, wavefunction, mine, swap(theirs, core))


def local(wavefunction, onsite_energy, left_env, right_env, source_device, source_block):
    owners = lax.axis_size("sector")
    sec, hops = source_device.shape
    fits = owners == 32 and sec <= 256 and (left_env.shape[0] + right_env.shape[0]) * hops <= 128
    fits = fits and (left_env.shape[1] - hops) % 2 == 0
    plan = spread_everywhere if fits and 2 * (sec * hops // owners) >= sec else ask_and_send
    return plan(wavefunction, onsite_energy, left_env, right_env, source_device, source_block)


def solution(mesh):
    return jax.shard_map(
        local,
        mesh=mesh,
        in_specs=(
            P(("groups", "sector"), None, None),
            P(("groups", "sector")),
            P(("groups", "sector"), None, None, None),
            P(("groups", "sector"), None, None, None),
            P(("groups", "sector"), None),
            P(("groups", "sector"), None),
        ),
        out_specs=(
            P(("groups", "sector"), None, None),
            P(("groups", "sector"), None, None),
            P("groups"),
        ),
        check_vma=False,
    )
```

```python
import functools

import jax
import jax.numpy as jnp
from jax import lax
from jax.experimental import pallas as pl
from jax.experimental.pallas import tpu as pltpu
from jax.sharding import PartitionSpec as P

F32 = jnp.float32
BF16 = jnp.bfloat16
VMEM_BYTES = 16 * 1024 * 1024
LOCAL_BYTES = 51 * 1024 * 1024
COST = pl.CostEstimate(flops=1, bytes_accessed=1, transcendentals=0)
ANY = pl.BlockSpec(memory_space=pl.ANY)
VMEM = pl.BlockSpec(memory_space=pltpu.VMEM)
HBM = pl.BlockSpec(memory_space=pltpu.HBM)
SMEM = pl.BlockSpec(memory_space=pltpu.SMEM)
TOKEN = jax.ShapeDtypeStruct((8, 128), F32)


def dot(a, b):
    return jnp.dot(a, b, preferred_element_type=F32)


def earlier_count(targets):
    length = targets.shape[0]
    row_iota = lax.broadcasted_iota(jnp.int32, (length, length), 0)
    col_iota = lax.broadcasted_iota(jnp.int32, (length, length), 1)
    earlier = (targets[:, None] == targets[None, :]) & (col_iota < row_iota)
    return jnp.sum(earlier.astype(jnp.int32), axis=1)


def ask_and_send(wavefunction, onsite_energy, left_env, right_env, source_device, source_block):
    owners = lax.axis_size("sector")
    sec_dev, block_size = wavefunction.shape[:2]
    left_count, channels = left_env.shape[:2]
    right_count = right_env.shape[0]
    hop_count = source_device.shape[1]
    local_count = channels - hop_count
    capacity = sec_dev * hop_count // owners
    targets = source_device.reshape(-1)
    slot_index = targets * capacity + earlier_count(targets)
    asked_for = jnp.zeros((owners * capacity,), jnp.int32).at[slot_index].set(source_block.reshape(-1))
    asked_for = lax.all_to_all(asked_for.reshape(owners, capacity), "sector", 0, 0, tiled=True)
    received = lax.all_to_all(wavefunction[asked_for], "sector", 0, 0, tiled=True)
    fetched = received.reshape(owners * capacity, block_size, block_size)[slot_index]
    fetched = fetched.reshape(left_count, right_count, hop_count, block_size, block_size)
    grid = wavefunction.reshape(left_count, right_count, 1, block_size, block_size)
    spread_out = jnp.broadcast_to(grid, (left_count, right_count, local_count, block_size, block_size))
    inputs_all = jnp.concatenate([spread_out, fetched], axis=2)
    middle = jnp.einsum("ijhab,jhbc->ijhac", inputs_all, right_env, preferred_element_type=F32).astype(BF16)
    summed = jnp.einsum("ihxa,ijhac->ijxc", left_env, middle, preferred_element_type=F32)
    psi_float = wavefunction.astype(F32)
    hpsi = summed.reshape(sec_dev, block_size, block_size) + onsite_energy[:, None, None] * psi_float
    numerator, denominator = lax.psum((jnp.sum(psi_float * hpsi), jnp.sum(psi_float * psi_float)), "sector")
    quotient = numerator / denominator
    residual = (hpsi - quotient * psi_float).astype(BF16)
    return hpsi.astype(BF16), residual, quotient.reshape(1)


def local_kernel(psi, right, left, acc, square, moved, psi_buf, r_buf, l_buf, middle, sems, moved_sems):
    rows, cols, size = psi.shape[0], psi.shape[1], psi.shape[2]
    chans = r_buf.shape[1]
    hops = right.shape[1] - chans
    psi_copy = pltpu.make_async_copy(psi, psi_buf, sems.at[0, 0])
    r_copy = [pltpu.make_async_copy(right.at[j, pl.ds(0, chans)], r_buf.at[j], sems.at[1, j]) for j in range(cols)]
    l_copy = [pltpu.make_async_copy(left.at[i, pl.ds(0, chans)], l_buf.at[i], sems.at[2, i]) for i in range(rows)]
    parts = [right.at[j, pl.ds(chans, hops)] for j in range(cols)] + [left.at[i, pl.ds(chans, hops)] for i in range(rows)]
    for n, part in enumerate(parts):
        parts[n] = pltpu.make_async_copy(part, moved.at[pl.ds(n * hops, hops)], moved_sems.at[n])
    for copy in [psi_copy] + r_copy + l_copy:
        copy.start()
    psi_copy.wait()
    for j in range(cols):
        r_copy[j].wait()
        if j == 1:
            for part in parts:
                part.start()
        column = psi_buf[:, j].reshape(rows * size, size)
        for h in range(0, chans, 2):
            pair = jnp.concatenate([r_buf[j, h], r_buf[j, h + 1]], axis=1)
            product = dot(column, pair).astype(BF16)
            for i in range(rows):
                for g in range(2):
                    block = product[i * size : (i + 1) * size, g * size : (g + 1) * size]
                    middle[i, pl.ds((h + g) * size, size), pl.ds(j * size, size)] = block
    total = jnp.zeros((size, size), F32)
    first = (rows + cols) * hops
    for i in range(rows):
        l_copy[i].wait()
        wide = jnp.concatenate([l_buf[i, h] for h in range(chans)], axis=1)
        summed = dot(wide, middle[i])
        for j in range(cols):
            moved[first + i * cols + j] = psi_buf[i, j]
            block = psi_buf[i, j].astype(F32)
            acc[i * cols + j] = summed[:, j * size : (j + 1) * size]
            total += block * block
    square[...] = total
    for part in parts:
        part.wait()


def local_call(psi, right, left, hops):
    sec, size = psi.shape[:2]
    rows, cols, chans = left.shape[0], right.shape[0], left.shape[1] - hops
    return pl.pallas_call(
        local_kernel,
        out_shape=(
            jax.ShapeDtypeStruct((sec, size, size), F32),
            jax.ShapeDtypeStruct((size, size), F32),
            jax.ShapeDtypeStruct(((rows + cols) * hops + sec, size, size), BF16),
        ),
        in_specs=[HBM] * 3,
        out_specs=[VMEM] * 3,
        scratch_shapes=[
            pltpu.VMEM((rows, cols, size, size), BF16),
            pltpu.VMEM((cols, chans, size, size), BF16),
            pltpu.VMEM((rows, chans, size, size), BF16),
            pltpu.VMEM((rows, chans * size, cols * size), BF16),
            pltpu.SemaphoreType.DMA((3, max(rows, cols, 2))),
            pltpu.SemaphoreType.DMA((rows + cols,)),
        ],
        compiler_params=pltpu.CompilerParams(vmem_limit_bytes=LOCAL_BYTES),
        cost_estimate=COST,
        name="local_channels",
    )(psi.reshape(rows, cols, size, size), right, left)


def hop_kernel(base, count, first, diagonal, tally, last, capacity, *refs):
    refs = list(refs)
    take = lambda n: [refs.pop(0) for _ in range(n)]
    order, *terms = take(3)
    envs = take(2 if first else 1)
    acc_in = take(1 if first else 2)
    bufs = take(count)
    onsite = take(1)[0] if diagonal else None
    tally_in = take(1)[0] if tally == "add" else None
    square = take(1)[0] if last else None
    acc = take(2)
    sums = take(1)[0]
    env = take(1)[0] if first else envs[0]
    (sems,) = refs
    fills = [pltpu.make_async_copy(envs[e], env.at[e], sems.at[e]) for e in range(2)] if first else []
    if first:
        fills.append(pltpu.make_async_copy(acc_in[0], acc[0], sems.at[2]))
        for fill in fills:
            fill.start()
        acc[1][...] = jnp.zeros(acc[1].shape, F32)
    else:
        for e in range(2):
            acc[e][...] = acc_in[e][...]
    for fill in fills:
        fill.wait()
    sec = acc[0].shape[0]
    first_psi = env.shape[1] - sec
    if diagonal:
        for t in range(sec):
            acc[0][t] = acc[0][t] + onsite[t] * env[0, first_psi + t].astype(F32)
    total = tally_in[...] if tally == "add" else jnp.zeros(acc[0].shape[1:], F32)
    for s, psi in enumerate(bufs):
        slot = order[base + s] * capacity
        words = [(e, terms[e][slot + r]) for e in range(2) for r in range(capacity)]
        mids = [dot(psi[w & 255], env[e, (w >> 16) & 255]).astype(BF16) for e, w in words]
        parts = [dot(env[e, w >> 24], mid) for (e, w), mid in zip(words, mids)]
        for (e, w), part in zip(words, parts):
            t = (w >> 8) & 255
            acc[e][t] = acc[e][t] + part
            if tally == "add":
                total += env[e, first_psi + t].astype(F32) * part
    if tally == "all":
        for e in range(2):
            total = lax.fori_loop(0, sec, lambda t, v, e=e: v + env[e, first_psi + t].astype(F32) * acc[e][t], total)
    if last:
        lanes = lax.broadcasted_iota(jnp.int32, sums.shape, 1)
        sums[...] = jnp.where(lanes < sums.shape[1] // 2, jnp.sum(total), jnp.sum(square[...]))
    elif tally:
        sums[...] = total
    else:
        sums[...] = jnp.zeros(sums.shape, F32)


def hop_call(name, order, base, terms, envs, accs, bufs, onsite, tally, tallies, square, owners, capacity):
    sec, size = accs[0].shape[:2]
    first, last = len(accs) == 1, bool(square)
    count = len(bufs)
    acc_shape = jax.ShapeDtypeStruct((sec, size, size), F32)
    side = (owners, size) if last else (size, size) if tally else (8, 128)
    out_shape = [acc_shape, acc_shape, jax.ShapeDtypeStruct(side, F32)]
    if first:
        out_shape.append(jax.ShapeDtypeStruct((2,) + envs[0].shape, BF16))
    return pl.pallas_call(
        functools.partial(hop_kernel, base, count, first, bool(onsite), tally, last, capacity),
        out_shape=out_shape,
        in_specs=[SMEM] * 3
        + [ANY if first else VMEM] * (len(envs) + len(accs))
        + [VMEM] * count
        + [SMEM] * len(onsite)
        + [VMEM] * len(tallies + square),
        out_specs=[VMEM] * len(out_shape),
        scratch_shapes=[pltpu.SemaphoreType.DMA((3,))],
        compiler_params=pltpu.CompilerParams(vmem_limit_bytes=VMEM_BYTES),
        cost_estimate=COST,
        name=name,
    )(order, *terms, *envs, *accs, *bufs, *onsite, *tallies, *square)


def hold_kernel(count, move, *refs):
    if move:
        src, dst = move
        flag, values, sem = refs[-count - 2], refs[: -count - 2], refs[-1]

        @pl.when(flag[0] != 0)
        def _():
            step = values[src].shape[0] // 4
            copies = []
            for n in range(4):
                part = pl.ds(n * step, step)
                copies.append(pltpu.make_async_copy(values[src].at[part], refs[dst - count - 1].at[part], sem.at[n]))
                copies[-1].start()
            for copy in copies:
                copy.wait()


def hold_until(values, tokens, move=None, flag=None):
    count = len(values)
    return pl.pallas_call(
        functools.partial(hold_kernel, count, move),
        out_shape=[jax.ShapeDtypeStruct(value.shape, value.dtype) for value in values],
        in_specs=[ANY] * (count + len(tokens)) + ([SMEM] if move else []),
        out_specs=[ANY] * count,
        scratch_shapes=[pltpu.SemaphoreType.DMA((4,))],
        input_output_aliases={n: n for n in range(count)},
        compiler_params=pltpu.CompilerParams(vmem_limit_bytes=VMEM_BYTES),
        cost_estimate=COST,
        name="hold",
    )(*values, *tokens, *([flag] if move else []))


def finish_kernel(sums, psi, mine, theirs, applied, residual, quotient):
    lanes = lax.broadcasted_iota(jnp.int32, sums.shape, 1)
    half = sums.shape[1] // 2
    ratio = jnp.sum(jnp.where(lanes == 0, sums[...], 0.0)) / jnp.sum(jnp.where(lanes == half, sums[...], 0.0))
    quotient[0] = ratio
    for t in range(psi.shape[0]):
        hpsi = mine[t] + theirs[t]
        applied[t] = hpsi.astype(BF16)
        residual[t] = (hpsi - ratio * psi[t].astype(F32)).astype(BF16)


def finish_call(sums, psi, mine, theirs):
    shape = jax.ShapeDtypeStruct(psi.shape, BF16)
    return pl.pallas_call(
        finish_kernel,
        out_shape=(shape, shape, jax.ShapeDtypeStruct((1,), F32)),
        in_specs=[VMEM] * 4,
        out_specs=(VMEM, VMEM, SMEM),
        compiler_params=pltpu.CompilerParams(vmem_limit_bytes=VMEM_BYTES),
        name="finish",
    )(sums, psi, mine, theirs)


def term_words(source_device, source_block, cols, capacity):
    sec, hops = source_device.shape
    targets = source_device.reshape(-1)
    slots = targets * capacity + earlier_count(targets)
    index = jnp.arange(sec * hops, dtype=jnp.int32)
    t, k = index // hops, index % hops
    right, left = (t % cols) * hops + k, (cols + t // cols) * hops + k
    words = source_block.reshape(-1) | (t << 8) | (right << 16) | (left << 24)
    hit = slots[None, :] == index[:, None]
    return jnp.sum(jnp.where(hit, words[None, :], 0), axis=1)


def spread_everywhere(wavefunction, onsite_energy, left_env, right_env, source_device, source_block):
    owners = lax.axis_size("sector")
    sec = wavefunction.shape[0]
    hops = source_device.shape[1]
    capacity = sec * hops // owners
    core, x, y, z = 1, 2, 4, 8
    xy = x ^ y
    layers = owners // z

    def swap(value, mask):
        return lax.ppermute(value, "sector", [(i, i ^ mask) for i in range(owners)])

    def swap_middle(value):
        pairs = []
        for i in range(owners):
            layer = i // z
            pairs.append((i, (layers - 1 - layer) * z + i % z if layer in (1, 2) else i ^ core))
        return lax.ppermute(value, "sector", pairs)

    me = lax.axis_index("sector")
    outer = ((me < z) | (me >= owners - z)).astype(jnp.int32).reshape(1)
    layer_masks = [0, z, 3 * z - outer * z, 2 * z + outer * z]
    groups = [
        [(0, 0), (0, x), (0, y), (1, 0), (0, xy), (1, y)],
        [(2, 0), (2, x), (2, y), (3, 0)],
        [(3, y), (3, x), (1, x)],
        [(1, xy), (2, xy), (3, xy)],
    ]
    order = jnp.concatenate([me ^ layer_masks[b] ^ jnp.full((1,), bits) for group in groups for b, bits in group])

    held = {(0, 0): wavefunction}
    state = {"base": 0}

    def hold(keys, *tokens, **move):
        held.update(zip(keys, hold_until([held[key] for key in keys], tokens, **move)))

    def run(group, onsite=(), tally=None, tallies=(), square=()):
        out = hop_call(
            f"hops_{group}", order, state["base"], terms, state["envs"], state["accs"],
            tuple(held[key] for key in groups[group]), onsite, tally, tallies, square, owners, capacity,
        )
        state["accs"] = out[:2]
        if group == 0:
            state["envs"] = out[3:]
        state["base"] += len(groups[group])
        return out[2]

    held[0, x], held[0, y] = swap(wavefunction, x), swap(wavefunction, y)
    held[1, 0] = swap(wavefunction, z)
    held["middle"] = swap_middle(wavefunction)
    terms = term_words(source_device, source_block, right_env.shape[0], capacity)
    terms = (terms, swap(terms, core))
    acc, square, held["env"] = local_call(wavefunction, right_env, left_env, hops)
    hold(["middle", (1, 0), (0, y), (0, x), "env"], terms[1])

    held[0, xy] = swap(held[0, y], x)
    held[1, y] = swap(held[1, 0], y)
    held["outer"] = swap(held["middle"], z)
    held["middle_2"] = swap_middle(held[1, 0])
    held["env_sib"] = swap(held["env"], core)
    hold(["middle"], held["outer"], move=(1, 0), flag=outer)
    hold(["env_sib", "middle", "middle_2", (1, y), (0, xy)])

    held[2, 0] = held["middle"]
    held[2, x], held[2, y] = swap(held[2, 0], x), swap(held[2, 0], y)
    held["outer_2"] = swap(held["middle_2"], z)
    state["accs"], state["envs"] = (acc,), (held["env"], held["env_sib"])
    done = run(0)
    hold(["middle_2", (0, x), (2, y), (2, x)], held["outer_2"], done, move=(4, 0), flag=outer)

    held[3, 0] = held["middle_2"]
    held[3, x], held[3, y] = swap(held[3, 0], x), swap(held[3, 0], y)
    held[1, x] = swap(held[0, x], z)
    done = run(1, (onsite_energy,))
    hold([(1, x), (2, y), (0, xy), (3, y), (3, x)], done)

    held[2, xy] = swap(held[2, y], x)
    held[3, xy] = swap(held[3, x], y)
    held[1, xy] = swap(held[0, xy], z)
    tally = run(2, (), "all")
    sums = run(3, (), "add", (tally,), (square,))
    sums = lax.all_to_all(sums, "sector", 0, 0, tiled=True)
    mine, theirs = state["accs"]
    return finish_call(sums, wavefunction, mine, swap(theirs, core))


def local(wavefunction, onsite_energy, left_env, right_env, source_device, source_block):
    owners = lax.axis_size("sector")
    sec, hops = source_device.shape
    fits = owners == 32 and sec <= 256 and (left_env.shape[0] + right_env.shape[0]) * hops <= 128
    fits = fits and (left_env.shape[1] - hops) % 2 == 0
    plan = spread_everywhere if fits and 2 * (sec * hops // owners) >= sec else ask_and_send
    return plan(wavefunction, onsite_energy, left_env, right_env, source_device, source_block)


def solution(mesh):
    return jax.shard_map(
        local,
        mesh=mesh,
        in_specs=(
            P(("groups", "sector"), None, None),
            P(("groups", "sector")),
            P(("groups", "sector"), None, None, None),
            P(("groups", "sector"), None, None, None),
            P(("groups", "sector"), None),
            P(("groups", "sector"), None),
        ),
        out_specs=(
            P(("groups", "sector"), None, None),
            P(("groups", "sector"), None, None),
            P("groups"),
        ),
        check_vma=False,
    )
```
